32 devices in a mesh: dp: 4 (over x, core), fsdp: 8 (over z, y).
Axes of the slice: x: 2, y: 2, z: 4, core: 2. Of those that a mesh axis runs over, the one named last changes fastest.
Arguments:
- attn_heads: bfloat16 [64, 4096], P('dp', 'fsdp'), may hold values from -6 to 6
- out_proj: bfloat16 [4096, 4608], P('fsdp'), may hold values from -0.09375 to 0.09375
- resid_pre: bfloat16 [64, 4608], P(('dp', 'fsdp')), may hold values from -25 to 25
- post_gain: float32 [4608], replicated, may hold values from 0.5 to 1.5
- enc_weight: bfloat16 [4608, 65536], P(None, ('dp', 'fsdp')), may hold values from -0.09375 to 0.09375
- enc_bias: float32 [65536], P(('dp', 'fsdp')), may hold values from -3 to 3
- dec_weight: bfloat16 [65536, 4608], P(('dp', 'fsdp')), may hold values from -0.046875 to 0.046875
- dec_bias: float32 [4608], replicated, may hold values from -3 to 3
Outputs:
- enc_grad: bfloat16 [4608, 65536], P(None, ('dp', 'fsdp'))
- enc_bias_grad: float32 [65536], P(('dp', 'fsdp'))
- dec_grad: bfloat16 [65536, 4608], P(('dp', 'fsdp'))
- dec_bias_grad: float32 [4608], replicated
- loss: float32 [], replicated
The draws below stay inside these ranges and needn't reach their ends.
All inputs are finite; a program needn't handle non-finite values.
Results may differ from the reference program's by a relative error of at most 0.013.
Values may be sent and summed in bfloat16 or wider, within the bound.
No kernel may reach another device: no remote copies, remote signals or barrier semaphores. Data moves between devices by JAX's collectives and lax.ppermute only.
A program may use at most 128 MiB of HBM per device.

```python
import jax
import jax.numpy as jnp
from jax import lax

D = 4608
LAT = 65536
TOKENS = 64
ATTN = 4096


def draw_resid_pre(key, part):
    first, second = jax.random.split(key, 2)
    place = jnp.arange(TOKENS, dtype=jnp.float32) / max(TOKENS - 1, 1)
    rough = jnp.exp(jax.random.uniform(first, (TOKENS,), minval=-0.7, maxval=0.7))
    scale = (0.5 + 2.5 * place) * rough
    entries = jnp.clip(jax.random.normal(second, (TOKENS, D)), -4.0, 4.0)
    return jnp.clip(scale[:, None] * entries, -25.0, 25.0).astype(jnp.bfloat16)


def draw_dec_weight(key, part):
    first, second = jax.random.split(key, 2)
    place = jnp.arange(LAT, dtype=jnp.float32) / (LAT - 1)
    rough = jnp.exp(jax.random.uniform(first, (LAT,), minval=-0.7, maxval=0.7))
    scale = (0.5 + place) * rough
    entries = jnp.clip(jax.random.normal(second, (LAT, D)), -4.0, 4.0)
    limit = 12.0 * LAT ** (-0.5)
    return jnp.clip(scale[:, None] * entries * LAT ** (-0.5), -limit, limit).astype(jnp.bfloat16)


def steps_of(key, shape, cuts, low, top_value):
    gain, own = 1.0, jax.random.fold_in(key, 6)
    for dim, blocks in cuts:
        heights = jnp.exp(jax.random.uniform(jax.random.fold_in(own, dim), (blocks,), jnp.float32, low / len(cuts), top_value / len(cuts)))
        gain = gain * jnp.repeat(heights, shape[dim] // blocks).reshape([-1 if axis == dim else 1 for axis in range(len(shape))])
    return gain


def noise(key, shape, deviation, most, shards=(), kind=jnp.bfloat16):
    factor_of = steps_of(key, shape, shards, -0.22, 0.18) if shards else 1.0
    array = jax.random.normal(key, shape, jnp.float32) * deviation * factor_of
    return jnp.minimum(jnp.maximum(array, -most), most).astype(kind)


def setup_inputs(seed: int = 0) -> dict:
    arg_keys = jax.random.split(jax.random.key(seed), 9)
    attn_heads = noise(arg_keys[0], (TOKENS, ATTN), 1.0, 6.0, ((0, 4), (1, 8)))
    out_proj = noise(arg_keys[1], (ATTN, D), ATTN ** -0.5, 0.09375, ((0, 8),))
    resid_pre = draw_resid_pre(jax.random.fold_in(arg_keys[8], 71), 0)
    post_gain = jnp.clip(1.0 + 0.1 * jax.random.normal(arg_keys[3], (D,), jnp.float32), 0.5, 1.5)
    enc_weight = noise(arg_keys[4], (D, LAT), D ** -0.5, 0.09375, ((1, 32),))
    enc_bias = noise(arg_keys[5], (LAT,), 0.5, 3.0, ((0, 32),), jnp.float32)
    dec_weight = draw_dec_weight(jax.random.fold_in(arg_keys[8], 71), 0)
    dec_bias = noise(arg_keys[7], (D,), 0.5, 3.0, (), jnp.float32)
    return dict(attn_heads=attn_heads, out_proj=out_proj, resid_pre=resid_pre, post_gain=post_gain, enc_weight=enc_weight, enc_bias=enc_bias, dec_weight=dec_weight, dec_bias=dec_bias)


SPARSITY = 0.25
SMOOTHING = 0.1
EPSILON = 1e-06

def reference(attn_heads, out_proj, resid_pre, post_gain, enc_weight, enc_bias, dec_weight, dec_bias):
    projected = jnp.dot(attn_heads, out_proj, preferred_element_type=jnp.float32)
    scale = lax.rsqrt(lax.optimization_barrier(jnp.mean(projected * projected, axis=-1, keepdims=True)) + EPSILON)
    residual = (resid_pre.astype(jnp.float32) + projected * scale * post_gain).astype(jnp.bfloat16)
    preact = jnp.dot(residual, enc_weight, preferred_element_type=jnp.float32) + enc_bias
    latents = jnp.maximum(preact, 0.0)
    latents_b = latents.astype(jnp.bfloat16)
    dec_f = dec_weight.astype(jnp.float32)
    row_norms = jnp.sqrt(lax.optimization_barrier(jnp.sum(dec_f * dec_f, axis=1)) + EPSILON)
    recon = jnp.dot(latents_b, dec_weight, preferred_element_type=jnp.float32) + dec_bias
    error = recon - residual.astype(jnp.float32)
    error_sum = jnp.sum(error * error)
    penalty_sum = jnp.sum(latents * row_norms)
    loss = (0.5 * error_sum + SPARSITY * penalty_sum) / (residual.shape[0] * residual.shape[1])
    error_b = error.astype(jnp.bfloat16)
    dec_bias_grad = lax.optimization_barrier(jnp.sum(error_b.astype(jnp.float32), axis=0))
    usage = lax.optimization_barrier(jnp.sum(latents, axis=0))
    dec_grad = jnp.dot(latents_b.T, error_b, preferred_element_type=jnp.float32)
    dec_grad = (dec_grad + SPARSITY * (usage / row_norms)[:, None] * dec_f).astype(jnp.bfloat16)
    latent_grad = jnp.dot(error_b, dec_weight.T, preferred_element_type=jnp.float32) + SPARSITY * row_norms
    preact_grad = latent_grad * jax.nn.sigmoid(preact / SMOOTHING)
    enc_bias_grad = lax.optimization_barrier(jnp.sum(preact_grad, axis=0))
    enc_grad = jnp.dot(residual.T, preact_grad.astype(jnp.bfloat16), preferred_element_type=jnp.float32).astype(jnp.bfloat16)
    return (enc_grad, enc_bias_grad, dec_grad, dec_bias_grad, loss)
```

```python
import jax
import jax.numpy as jnp
from jax import lax
from jax.sharding import PartitionSpec as P

SPARSITY = 0.25
SMOOTHING = 0.1
EPSILON = 1e-06
F32 = jnp.float32
BF16 = jnp.bfloat16


class Split:
    def __init__(self, axis, length, inner, size):
        self.axis, self.length, self.inner, self.size = axis, length, inner, size

    def place(self):
        return (lax.axis_index(self.axis) // self.inner) % self.size

    def swap(self, x, k):
        pairs = []
        for i in range(self.length):
            a = (i // self.inner) % self.size
            pairs.append((i, i + ((a ^ k) - a) * self.inner))
        return lax.ppermute(x, self.axis, pairs)

    def scatter_sum(self, x):
        rows = x.shape[0] // self.size
        total = x[:rows].astype(F32)
        for k in range(1, self.size):
            total = total + self.swap(x[k * rows : (k + 1) * rows].astype(BF16), k).astype(F32)
        return total

    def gather(self, x):
        return jnp.concatenate([x] + [self.swap(x, k) for k in range(1, self.size)], axis=0)


def splits(mesh):
    dp, fsdp = mesh.shape["dp"], mesh.shape["fsdp"]
    cores = 2 if dp % 2 == 0 else 1
    deep = 4 if fsdp % 4 == 0 else 1
    return (
        Split("dp", dp, 1, cores),
        Split("dp", dp, cores, dp // cores),
        Split("fsdp", fsdp, fsdp // deep, deep),
        Split("fsdp", fsdp, 1, fsdp // deep),
    )


def all_sum(split, x):
    rows = x.shape[0] // split.size
    mine = x.astype(BF16)
    parts = [mine.astype(F32).reshape(split.size, rows, -1)]
    for k in range(1, split.size):
        got = split.swap(mine, k).astype(F32).reshape(split.size, rows, -1)
        parts.append(jnp.concatenate([got[j ^ k][None] for j in range(split.size)], axis=0))
    while len(parts) > 1:
        half = len(parts) // 2
        parts = [parts[i] + parts[i + half] for i in range(half)]
    return parts[0].reshape(x.shape)


def make_body(mesh):
    core, across, deep, side = splits(mesh)

    def body(attn_heads, out_proj, resid_pre, post_gain, enc_weight, enc_bias, dec_weight, dec_bias):
        own = resid_pre.shape[0]
        heads = attn_heads.reshape(deep.size, side.size, own, -1)
        heads = jnp.take(heads, jnp.arange(deep.size) ^ deep.place(), axis=0)
        heads = jnp.take(heads, jnp.arange(side.size) ^ side.place(), axis=1)
        heads = heads.reshape(attn_heads.shape)
        resid_rows = side.gather(resid_pre)
        partial = jnp.dot(heads, out_proj, preferred_element_type=F32)
        projected = all_sum(side, deep.scatter_sum(partial))
        scale = lax.rsqrt(jnp.mean(projected * projected, axis=-1, keepdims=True) + EPSILON)
        resid_own = (resid_rows.astype(F32) + projected * scale * post_gain).astype(BF16)
        resid_all = core.gather(across.gather(deep.gather(resid_own)))

        preact = jnp.dot(resid_all, enc_weight, preferred_element_type=F32) + enc_bias
        latents = jnp.maximum(preact, 0.0)
        latents_b = latents.astype(BF16)
        row_norms = jnp.sqrt(jnp.sum(jnp.square(dec_weight.astype(F32)), axis=1) + EPSILON)
        penalty = jnp.full((8, 128), jnp.sum(latents * row_norms), F32)
        for split in (core, across, deep, side):
            k = 1
            while k < split.size:
                penalty = penalty + split.swap(penalty, k)
                k *= 2

        recon = jnp.dot(latents_b, dec_weight, preferred_element_type=F32)
        recon = all_sum(side, deep.scatter_sum(across.scatter_sum(core.scatter_sum(recon))))
        error_own = (recon + dec_bias - resid_own.astype(F32)).astype(BF16)
        error_b = core.gather(across.gather(deep.gather(error_own)))
        error_f = error_b.astype(F32)
        order = error_f.reshape(core.size, across.size, deep.size, side.size, own, -1)
        total = order
        for split in (core, across, deep, side):
            n = split.size
            while n > 1:
                total = total[: n // 2] + total[n // 2 :]
                n //= 2
            total = total[0]
        columns = jnp.sum(total, axis=0)
        squares = order * order
        for split in (core, across, deep, side):
            n = split.size
            while n > 1:
                squares = squares[: n // 2] + squares[n // 2 :]
                n //= 2
            squares = squares[0]
        loss = (0.5 * jnp.sum(squares) + SPARSITY * penalty[0, 0]) / error_b.size

        usage = jnp.sum(latents, axis=0)
        dec_grad = lax.dot_general(latents_b, error_b, (((0,), (0,)), ((), ())), preferred_element_type=F32)
        dec_grad = (dec_grad + SPARSITY * (usage / row_norms)[:, None] * dec_weight.astype(F32)).astype(BF16)
        latent_grad = lax.dot_general(error_b, dec_weight, (((1,), (1,)), ((), ())), preferred_element_type=F32)
        latent_grad = latent_grad + SPARSITY * row_norms
        preact_grad = latent_grad * jax.nn.sigmoid(preact / SMOOTHING)
        enc_bias_grad = jnp.sum(preact_grad, axis=0)
        enc_grad = lax.dot_general(
            resid_all, preact_grad.astype(BF16), (((0,), (0,)), ((), ())), preferred_element_type=F32
        ).astype(BF16)
        return (enc_grad, enc_bias_grad, dec_grad, columns, loss)

    return body


def solution(mesh):
    placed = (
        P("dp", "fsdp"),
        P("fsdp", None),
        P(("dp", "fsdp"), None),
        P(),
        P(None, ("dp", "fsdp")),
        P(("dp", "fsdp")),
        P(("dp", "fsdp"), None),
        P(),
    )
    return jax.shard_map(
        make_body(mesh),
        mesh=mesh,
        in_specs=placed,
        out_specs=(P(None, ("dp", "fsdp")), P(("dp", "fsdp")), P(("dp", "fsdp"), None), P(), P()),
        check_vma=False,
    )
```

```python
import functools
import itertools
import math

import jax
import jax.numpy as jnp
from jax import lax
from jax.experimental import pallas as pl
from jax.experimental.pallas import tpu as pltpu
from jax.sharding import PartitionSpec as P

SPARSITY = 0.25
SMOOTHING = 0.1
EPSILON = 1e-06
F32 = jnp.float32
BF16 = jnp.bfloat16
LANES = 128
PIECES = 4


class Split:
    def __init__(self, axis, inner, size):
        self.axis, self.inner, self.size = axis, inner, size

    def place(self):
        return (lax.axis_index(self.axis) // self.inner) % self.size


class Group:
    def __init__(self, mesh, *splits):
        self.lengths = {axis: mesh.shape[axis] for axis in ("dp", "fsdp")}
        self.splits = splits
        self.size = math.prod(s.size for s in splits)
        self.keys = list(itertools.product(*(range(s.size) for s in splits)))

    def swap(self, x, key):
        pairs = []
        for d in range(self.lengths["dp"]):
            for f in range(self.lengths["fsdp"]):
                to = {"dp": d, "fsdp": f}
                for split, k in zip(self.splits, key):
                    a = (to[split.axis] // split.inner) % split.size
                    to[split.axis] += ((a ^ k) - a) * split.inner
                width = self.lengths["fsdp"]
                pairs.append((d * width + f, to["dp"] * width + to["fsdp"]))
        return lax.ppermute(x, ("dp", "fsdp"), pairs)

    def swaps(self, pieces):
        return [self.swap(p, key) for p, key in zip(pieces, self.keys[1:])]

    def spread(self, x):
        return [x] + [self.swap(x, key) for key in self.keys[1:]]


def block_of(total, most):
    return max(b for b in range(LANES, most + 1, LANES) if total % b == 0)


def resident(count):
    return [pl.BlockSpec(memory_space=pltpu.VMEM)] * count


def anywhere(count):
    return [pl.BlockSpec(memory_space=pl.ANY)] * count


def in_hbm(x):
    return pltpu.with_memory_space_constraint(x, pltpu.HBM)


def in_vmem(x):
    return pltpu.with_memory_space_constraint(x, pltpu.VMEM)


def params(megabytes):
    return pltpu.CompilerParams(vmem_limit_bytes=megabytes * 1024 * 1024)


def cost(flops, count):
    return pl.CostEstimate(flops=flops, bytes_accessed=count, transcendentals=0)


def struct(shape, kind):
    return jax.ShapeDtypeStruct(shape, kind)


def small(kernel, outs, *args, name):
    count = sum(x.size * x.dtype.itemsize for x in args) + sum(o.size * o.dtype.itemsize for o in outs)
    return pl.pallas_call(
        kernel,
        in_specs=resident(len(args)),
        out_specs=resident(len(outs)),
        out_shape=list(outs),
        compiler_params=params(6),
        cost_estimate=cost(count, count),
        name=name,
    )(*args)


def project(heads, weight, resid, gain, bias, deep, side):
    tokens = heads.shape[0]
    features = weight.shape[1]
    rows = tokens // side.size
    own = rows // deep.size
    quarter = features // deep.size
    shift = own.bit_length() - 1

    def kernel(heads, weight, resid, gain, bias, packed, gain_row, bias_row, keep, *send):
        to = lax.broadcasted_iota(jnp.int32, (tokens, tokens), 0)
        source = lax.broadcasted_iota(jnp.int32, (tokens, tokens), 1)
        across = lax.shift_right_logical(to, (rows.bit_length() - 1)) ^ side.place()
        down = (lax.shift_right_logical(to, shift) & (deep.size - 1)) ^ deep.place()
        wanted = (down * side.size + across) * own + (to & (own - 1))
        pick = jnp.where(source == wanted, 1.0, 0.0).astype(BF16)
        turned = jnp.dot(pick, heads[...], preferred_element_type=F32).astype(BF16)
        part = jnp.dot(turned, weight[...], preferred_element_type=F32)
        keep[...] = part[:rows]
        for k in range(1, side.size):
            send[k - 1][...] = part[k * rows : (k + 1) * rows].astype(BF16)

        @pl.when(pl.program_id(0) == 0)
        def _():
            values = resid[...].astype(F32)
            pieces = [values[:, q * quarter : (q + 1) * quarter] for q in range(deep.size)]
            packed[...] = jnp.concatenate(pieces, axis=0).astype(BF16)
            gain_row[...] = gain[...].reshape(1, features)
            bias_row[...] = bias[...].reshape(1, features)

    wide = block_of(features, 1536)
    fixed = lambda shape: pl.BlockSpec(shape, lambda i: (0,) * len(shape))
    spec = pl.BlockSpec((rows, wide), lambda i: (0, i))
    return pl.pallas_call(
        kernel,
        grid=(features // wide,),
        in_specs=[
            fixed(heads.shape),
            pl.BlockSpec((weight.shape[0], wide), lambda i: (0, i)),
            fixed(resid.shape),
            fixed(gain.shape),
            fixed(bias.shape),
        ],
        out_specs=[fixed((rows, quarter)), fixed((1, features)), fixed((1, features))] + [spec] * side.size,
        out_shape=[struct((rows, quarter), BF16), struct((1, features), F32), struct((1, features), F32)]
        + [struct((rows, features), F32)]
        + [struct((rows, features), BF16)] * (side.size - 1),
        compiler_params=params(12),
        cost_estimate=cost(2 * tokens * weight.size, 2 * weight.size),
        name="project",
    )(in_hbm(heads), in_hbm(weight), in_hbm(resid), in_hbm(gain), in_hbm(bias))


def add_up(keep, got, parts, kind, name, beside=None, after=()):
    rows, columns = keep.shape
    part = rows // parts
    extra = [] if beside is None else [beside]
    width = columns + sum(b.shape[1] for b in extra)

    def kernel(*refs):
        ins, outs = refs[: 1 + len(got)], refs[-parts:]
        for p in range(parts):
            at = slice(p * part, (p + 1) * part)
            total = ins[0][at, :]
            for g in ins[1:]:
                total = total + g[at, :].astype(F32)
            outs[p][:, :columns] = total.astype(outs[p].dtype)
        if extra:
            outs[0][:, columns:] = refs[1 + len(got)][...]

    outs = [struct((part, width), kind)] + [struct((part, columns), BF16)] * (parts - 1)
    return small(kernel, outs, keep, *got, *extra, *after, name=name)


def group_sum(parts, own):
    size = len(parts)
    terms = []
    for k, part in enumerate(parts):
        pieces = [part[(j ^ k) * own : ((j ^ k) + 1) * own, :] for j in range(size)]
        terms.append(jnp.concatenate(pieces, axis=0) if size > 1 else part)
    while len(terms) > 1:
        half = len(terms) // 2
        terms = [terms[i] + terms[i + half] for i in range(half)]
    return terms[0]


def residual(parts, gain, after):
    rows = parts[0].shape[0]
    features = gain.shape[1]
    count = len(parts)
    own, quarter = rows // count, features // count

    def kernel(*refs):
        sums, gain, out = refs[:count], refs[count], refs[-1]
        projected = group_sum([p[:, :features].astype(F32) for p in sums], own)
        scale = lax.rsqrt(jnp.mean(projected * projected, axis=-1, keepdims=True) + EPSILON)
        packed = [p[:, features:].astype(F32) for p in sums]
        for q in range(count):
            at = slice(q * quarter, (q + 1) * quarter)
            before = jnp.concatenate([p[q * own : (q + 1) * own, :] for p in packed], axis=0)
            out[:, at] = (before + projected[:, at] * scale * gain[:, at]).astype(BF16)

    return small(kernel, [struct((rows, features), BF16)], *parts, gain, *after, name="residual")[0]


def error_of(parts, resid, bias):
    rows, columns = parts[0].shape
    features = resid.shape[1]
    own = rows // len(parts)

    def kernel(*refs):
        sums, resid, bias, out = refs[: len(parts)], refs[-3], refs[-2], refs[-1]
        total = group_sum([p[...].astype(F32) for p in sums], own)
        out[:, :features] = (total[:, :features] + bias[...] - resid[...].astype(F32)).astype(BF16)
        out[:, features:] = total[:, features:].astype(BF16)

    return small(kernel, [struct((rows, columns), BF16)], *parts, resid, bias, name="error")[0]


def stack(pieces, name):
    rows, columns = pieces[0].shape

    def kernel(*refs):
        for i, ref in enumerate(refs[:-1]):
            refs[-1][i * rows : (i + 1) * rows, :] = ref[...]

    return small(kernel, [struct((rows * len(pieces), columns), pieces[0].dtype)], *pieces, name=name)[0]


def gather(stages, x):
    pieces = [x]
    for group in reversed(stages):
        if len(pieces) > 4:
            pieces = [stack(pieces, "gathered")]
        pieces = pieces + [group.swap(p, key) for key in group.keys[1:] for p in pieces]
    return pieces


def load(items, after, name):
    chunks = []
    for n, (_, first, rows, _) in enumerate(items):
        step = block_of(rows, 384) if rows % LANES == 0 else rows
        chunks += [(n, first + r, r, step) for r in range(0, rows, step)]
    outs, places = [], []
    for source, _, rows, norms in items:
        places.append(len(outs))
        outs.append(pltpu.VMEM((rows, source.shape[1]), source.dtype))
        if norms:
            outs += [struct((rows, 1), F32), struct((1, rows), F32)]
    outs.append(struct((8, LANES), F32))

    def kernel(*refs):
        sources, results, sems = refs[: len(items)], refs[len(items) + 1 : -1], refs[-1]
        copies = []
        for i, (n, at, to, step) in enumerate(chunks):
            copies.append(
                pltpu.make_async_copy(
                    sources[n].at[pl.ds(at, step)], results[places[n]].at[pl.ds(to, step)], sems.at[i]
                )
            )
            copies[-1].start()
        for copy, (n, _, to, step) in zip(copies, chunks):
            copy.wait()
            if items[n][3]:
                row_norms(*results[places[n] : places[n] + 3], to, step)
        results[-1][...] = jnp.zeros_like(results[-1])

    found = pl.pallas_call(
        kernel,
        in_specs=anywhere(len(items)) + resident(1),
        out_specs=resident(len(outs)),
        out_shape=outs,
        scratch_shapes=[pltpu.SemaphoreType.DMA((len(chunks),))],
        compiler_params=params(4),
        cost_estimate=cost(0, sum(2 * rows * source.shape[1] for source, _, rows, _ in items)),
        name=name,
    )(*[in_hbm(item[0]) for item in items], after)
    return found


def row_norms(weight, norm, norm_row, first, rows):
    features = weight.shape[1]
    at = slice(first, first + rows)
    squares = jnp.zeros((rows, LANES), F32)
    for c in range(0, features, LANES):
        w = weight[at, c : c + LANES].astype(F32)
        squares = squares + w * w
    value = jnp.sqrt(jnp.sum(squares, axis=1, keepdims=True) + EPSILON)
    norm[at, :] = value
    norm_row[:, at] = jnp.broadcast_to(value, (rows, LANES)).T[:1, :]


def encode(parts, early, weight, bias):
    rows = parts[0].shape[0]
    tokens = sum(p.shape[0] for p in parts)
    features, latents = weight.shape
    depth = features // PIECES
    late = PIECES - len(early)
    wide = block_of(latents, 256)

    def kernel(*refs):
        parts_in, early_in = refs[: len(parts)], refs[len(parts) : len(parts) + len(early)]
        weight, bias, preact, resid, held, sems = refs[len(parts) + len(early) :]
        copies = []
        for i in range(late):
            at = pl.ds((len(early) + i) * depth, depth)
            copies.append(pltpu.make_async_copy(weight.at[at], held.at[i], sems.at[i]))
            copies[-1].start()
        for i, part in enumerate(parts_in):
            resid[i * rows : (i + 1) * rows, :] = part[...]
        row = bias[...].reshape(1, latents)
        for c in range(0, latents, wide):
            at = slice(c, c + wide)
            total = row[:, at]
            for i, w in enumerate(early_in):
                total = total + jnp.dot(
                    resid[:, i * depth : (i + 1) * depth], w[:, at], preferred_element_type=F32
                )
            preact[:, at] = jnp.broadcast_to(total, (tokens, wide))
        for i, copy in enumerate(copies):
            copy.wait()
            k = len(early) + i
            for c in range(0, latents, wide):
                at = slice(c, c + wide)
                preact[:, at] += jnp.dot(
                    resid[:, k * depth : (k + 1) * depth], held[i, :, at], preferred_element_type=F32
                )

    return pl.pallas_call(
        kernel,
        in_specs=resident(len(parts) + len(early)) + anywhere(1) + resident(1),
        out_specs=resident(2),
        out_shape=[struct((tokens, latents), F32), struct((tokens, features), BF16)],
        scratch_shapes=[pltpu.VMEM((max(late, 1), depth, latents), BF16), pltpu.SemaphoreType.DMA((max(late, 1),))],
        compiler_params=params(18),
        cost_estimate=cost(2 * tokens * features * latents, 2 * tokens * features),
        name="encode",
    )(*parts, *[in_vmem(e) for e in early], in_hbm(weight), bias)


def decode_kernel(count, preact, *refs):
    weights, norm_cols, norm_rows = refs[:count], refs[count : 2 * count], refs[2 * count : 3 * count]
    keep, send, latents_t, coef, latents_b = refs[3 * count :]
    tokens = preact.shape[0]
    features = weights[0].shape[1]
    half = keep.shape[0]
    penalty = jnp.zeros((tokens, 1), F32)
    spans, start = [], 0
    for p in range(count):
        piece = weights[p].shape[0]
        spans.append(slice(start, start + piece))
        rows = block_of(piece, 256) if piece % LANES == 0 else piece
        for r in range(0, piece, rows):
            at, inside = slice(start + r, start + r + rows), slice(r, r + rows)
            latents = jnp.maximum(preact[:, at], 0.0)
            latents_b[:, at] = latents.astype(BF16)
            turned = latents.T
            latents_t[at, :] = turned.astype(BF16)
            coef[at, :] = SPARSITY * (jnp.sum(turned, axis=1, keepdims=True) / norm_cols[p][inside, :])
            penalty = penalty + jnp.sum(latents * norm_rows[p][:, inside], axis=1, keepdims=True)
        start += piece
    keep[:, features:] = jnp.broadcast_to(penalty[:half], (half, LANES))
    if half < tokens:
        send[:, features:] = jnp.broadcast_to(penalty[half:], (tokens - half, LANES)).astype(BF16)
    wide = block_of(features, 512)
    for c in range(0, features, wide):
        at = slice(c, c + wide)
        part = jnp.dot(latents_b[:, spans[0]], weights[0][:, at], preferred_element_type=F32)
        for p in range(1, count):
            part = part + jnp.dot(latents_b[:, spans[p]], weights[p][:, at], preferred_element_type=F32)
        keep[:, at] = part[:half]
        if half < tokens:
            send[:, at] = part[half:].astype(BF16)


def decode(preact, weights, norm_cols, norm_rows, parts):
    tokens, latents = preact.shape
    features = weights[0].shape[1]
    kept = tokens // parts
    sent = max(tokens - kept, 8)
    return pl.pallas_call(
        functools.partial(decode_kernel, len(weights)),
        in_specs=resident(1 + 3 * len(weights)),
        out_specs=resident(4),
        out_shape=[
            struct((kept, features + LANES), F32),
            struct((sent, features + LANES), BF16),
            struct((latents, tokens), BF16),
            struct((latents, 1), F32),
        ],
        scratch_shapes=[pltpu.VMEM((tokens, latents), BF16)],
        compiler_params=params(12),
        cost_estimate=cost(2 * tokens * features * latents, 6 * tokens * features),
        name="decode",
    )(preact, *[in_vmem(w) for w in weights], *norm_cols, *norm_rows)


def turn(x, after):
    def kernel(x, after, out):
        out[...] = x[...].astype(F32).T.astype(BF16)

    return small(kernel, [struct(x.shape[::-1], BF16)], x, after, name="turn")[0]


def fold(x):
    n = x.shape[0]
    while n > 1 and n % 2 == 0:
        n //= 2
        x = x[:n] + x[n:]
    return x if n == 1 else jnp.sum(x, axis=0, keepdims=True)


def grad_kernel(pieces, count, *refs):
    parts, weights, norm_rows = refs[:pieces], refs[pieces : pieces + count], refs[pieces + count : pieces + 2 * count]
    (resid_t, preact, latents_t, coef, dec_grad, enc_grad, bias_grad, column_sum, loss,
     error, error_t, dec_stage, enc_stage, dec_sem, enc_sem) = refs[pieces + 2 * count :]
    height = parts[0].shape[0]
    for i, part in enumerate(parts):
        error[i * height : (i + 1) * height, :] = part[...]
    tokens = error.shape[0]
    latents = latents_t.shape[0]
    features = weights[0].shape[1]
    dec_slots, rows = dec_stage.shape[:2]
    enc_slots, deep, span = enc_stage.shape
    wide = block_of(features, 512)
    where = [(p, r) for p in range(count) for r in range(0, weights[p].shape[0], rows)]
    dec_copies, enc_copies = [], []

    def outer(i):
        p, r = where[i]
        at, inside = slice(i * rows, (i + 1) * rows), slice(r, r + rows)
        if i >= dec_slots:
            dec_copies[i - dec_slots].wait()
        slot = i % dec_slots
        scale = coef[at, :]
        for c in range(0, features, wide):
            over = slice(c, c + wide)
            product = jnp.dot(latents_t[at, :], error[:, over], preferred_element_type=F32)
            product = product + scale * weights[p][inside, over].astype(F32)
            dec_stage[slot, :, over] = product.astype(BF16)
        copy = pltpu.make_async_copy(dec_stage.at[slot], dec_grad.at[pl.ds(i * rows, rows)], dec_sem.at[slot])
        copy.start()
        dec_copies.append(copy)

    def pull(i):
        p, r = where[i]
        at, inside = slice(i * rows, (i + 1) * rows), slice(r, r + rows)
        back = jnp.dot(weights[p][inside, :], error_t[...], preferred_element_type=F32).T
        back = (back + SPARSITY * norm_rows[p][:, inside]) * jax.nn.sigmoid(preact[:, at] / SMOOTHING)
        bias_grad[:, at] = jnp.sum(back, axis=0, keepdims=True)
        return back.astype(BF16)

    def spread(first, pulled):
        for j in range(0, features, deep):
            n = len(enc_copies)
            if n >= enc_slots:
                enc_copies[n - enc_slots].wait()
            slot = n % enc_slots
            enc_stage[slot] = jnp.dot(resid_t[j : j + deep, :], pulled, preferred_element_type=F32).astype(BF16)
            copy = pltpu.make_async_copy(
                enc_stage.at[slot], enc_grad.at[pl.ds(j, deep), pl.ds(first, span)], enc_sem.at[slot]
            )
            copy.start()
            enc_copies.append(copy)

    outer(0)
    error_t[...] = error[:, :features].astype(F32).T.astype(BF16)
    each = span // rows
    for i in range(0, latents // rows, each):
        pulled = []
        for k in range(i, i + each):
            if k:
                outer(k)
            pulled.append(pull(k))
        spread(i * rows, jnp.concatenate(pulled, axis=1) if each > 1 else pulled[0])

    squares = jnp.zeros((1, wide), F32)
    for c in range(0, features, wide):
        e = error[:, c : c + wide].astype(F32)
        column_sum[:, c : c + wide] = fold(e)
        squares = squares + fold(e * e)
    squared = jnp.sum(squares, axis=1, keepdims=True)
    penalty = fold(error[:, features:].astype(F32))
    loss[...] = (0.5 * squared + SPARSITY * penalty) / (tokens * features)
    for copy in dec_copies[-dec_slots:] + enc_copies[-enc_slots:]:
        copy.wait()


def gradients(parts, resid_t, preact, latents_t, coef, weights, norm_rows):
    tokens, latents = preact.shape
    features = weights[0].shape[1]
    rows = math.gcd(*[w.shape[0] for w in weights], 256)
    span = math.gcd(latents, 512)
    deep = block_of(features, 1152)
    return pl.pallas_call(
        functools.partial(grad_kernel, len(parts), len(weights)),
        in_specs=resident(len(parts) + 2 * len(weights) + 4),
        out_specs=anywhere(2) + resident(3),
        out_shape=[
            struct((latents, features), BF16),
            struct((features, latents), BF16),
            struct((1, latents), F32),
            struct((1, features), F32),
            struct((1, LANES), F32),
        ],
        scratch_shapes=[
            pltpu.VMEM((tokens, features + LANES), BF16),
            pltpu.VMEM((features, tokens), BF16),
            pltpu.VMEM((3, rows, features), BF16),
            pltpu.VMEM((4, deep, span), BF16),
            pltpu.SemaphoreType.DMA((3,)),
            pltpu.SemaphoreType.DMA((4,)),
        ],
        compiler_params=params(24),
        cost_estimate=cost(6 * tokens * features * latents, 4 * features * latents),
        name="gradients",
    )(*parts, *[in_vmem(w) for w in weights], *norm_rows, resid_t, preact, latents_t, coef)


def make_body(mesh):
    dp, fsdp = mesh.shape["dp"], mesh.shape["fsdp"]
    cores = 2 if dp % 2 == 0 else 1
    depth = 4 if fsdp % 4 == 0 else 1
    core_split, across_split = Split("dp", 1, cores), Split("dp", cores, dp // cores)
    deep_split, side_split = Split("fsdp", fsdp // depth, depth), Split("fsdp", 1, fsdp // depth)
    core, deep, side = Group(mesh, core_split), Group(mesh, deep_split), Group(mesh, side_split)
    if across_split.size * side_split.size <= 4:
        plane = [Group(mesh, across_split, side_split)]
    else:
        plane = [Group(mesh, across_split), side]
    stages = [core] + plane

    def body(attn_heads, out_proj, resid_pre, post_gain, enc_weight, enc_bias, dec_weight, dec_bias):
        latents, depth = dec_weight.shape[0], dec_weight.shape[1] // PIECES
        unit = 256 if latents % 2048 == 0 else LANES
        cut = max(latents // unit * 3 // 8, 1) * unit
        packed, gain, bias, keep, *send = project(
            attn_heads, out_proj, resid_pre, post_gain, dec_bias, deep_split, side_split
        )
        got = side.swaps(send)
        first = load([(dec_weight, 0, cut, True)], send[0] if send else keep, "load_first")
        summed = add_up(keep, got, 1, BF16, "heads_y", packed, first[-1:])[0]
        sums = deep.spread(summed)
        second = load(
            [(dec_weight, cut, latents - cut, True), (enc_weight, 0, depth, False)], summed, "load_second"
        )
        resid_own = residual(sums, gain, second[-1:])
        resid_parts = gather(stages, resid_own)
        third = load([(enc_weight, depth, depth, False)], resid_own, "load_third")
        early = [second[3], third[0]]
        held, norm_cols, norm_rows = [list(pair) for pair in zip(first[:3], second[:3])]

        preact, resid_all = encode(resid_parts, early, enc_weight, enc_bias)
        keep, send, latents_t, coef = decode(preact, held, norm_cols, norm_rows, core.size)
        send = [send]
        for i, group in enumerate(stages):
            last = i + 1 == len(stages)
            parts = 1 if last else stages[i + 1].size
            got = group.swaps(send)
            after = []
            if last:
                resid_t = turn(resid_all, send[0])
                after = [resid_t]
            keep, *send = add_up(keep, got, parts, BF16 if last else F32, "recon", None, after)
        error_own = error_of(deep.spread(keep), resid_own, bias)
        error_parts = gather(stages, error_own)

        dec_grad, enc_grad, bias_grad, column_sum, loss = gradients(
            error_parts, resid_t, preact, latents_t, coef, held, norm_rows
        )
        return (enc_grad, bias_grad.reshape(-1), dec_grad, column_sum.reshape(-1), loss[0, 0])

    return body


def solution(mesh):
    placed = (
        P("dp", "fsdp"),
        P("fsdp", None),
        P(("dp", "fsdp"), None),
        P(),
        P(None, ("dp", "fsdp")),
        P(("dp", "fsdp")),
        P(("dp", "fsdp"), None),
        P(),
    )
    return jax.shard_map(
        make_body(mesh),
        mesh=mesh,
        in_specs=placed,
        out_specs=(P(None, ("dp", "fsdp")), P(("dp", "fsdp")), P(("dp", "fsdp"), None), P(), P()),
        check_vma=False,
    )
```

```python
import functools
import itertools
import math

import jax
import jax.numpy as jnp
from jax import lax
from jax.experimental import pallas as pl
from jax.experimental.pallas import tpu as pltpu
from jax.sharding import PartitionSpec as P

SPARSITY = 0.25
SMOOTHING = 0.1
EPSILON = 1e-06
F32 = jnp.float32
BF16 = jnp.bfloat16
LANES = 128


class Split:
    def __init__(self, axis, inner, size):
        self.axis, self.inner, self.size = axis, inner, size

    def place(self):
        return (lax.axis_index(self.axis) // self.inner) % self.size


class Group:
    def __init__(self, mesh, *splits):
        self.lengths = {axis: mesh.shape[axis] for axis in ("dp", "fsdp")}
        self.splits = splits
        self.size = math.prod(s.size for s in splits)
        self.keys = list(itertools.product(*(range(s.size) for s in splits)))

    def swap(self, x, key):
        pairs = []
        for d in range(self.lengths["dp"]):
            for f in range(self.lengths["fsdp"]):
                to = {"dp": d, "fsdp": f}
                for split, k in zip(self.splits, key):
                    a = (to[split.axis] // split.inner) % split.size
                    to[split.axis] += ((a ^ k) - a) * split.inner
                width = self.lengths["fsdp"]
                pairs.append((d * width + f, to["dp"] * width + to["fsdp"]))
        return lax.ppermute(x, ("dp", "fsdp"), pairs)

    def swaps(self, pieces):
        return [self.swap(p, key) for p, key in zip(pieces, self.keys[1:])]

    def spread(self, x):
        return [x] + [self.swap(x, key) for key in self.keys[1:]]


def block_of(total, most):
    return max(b for b in range(LANES, most + 1, LANES) if total % b == 0)


def resident(count):
    return [pl.BlockSpec(memory_space=pltpu.VMEM)] * count


def anywhere(count):
    return [pl.BlockSpec(memory_space=pl.ANY)] * count


def in_hbm(x):
    return pltpu.with_memory_space_constraint(x, pltpu.HBM)


def in_vmem(x):
    return pltpu.with_memory_space_constraint(x, pltpu.VMEM)


def params(megabytes):
    return pltpu.CompilerParams(vmem_limit_bytes=megabytes * 1024 * 1024)


def cost(flops, count):
    return pl.CostEstimate(flops=flops, bytes_accessed=count, transcendentals=0)


def struct(shape, kind):
    return jax.ShapeDtypeStruct(shape, kind)


def small(kernel, outs, *args, name):
    count = sum(x.size * x.dtype.itemsize for x in args) + sum(o.size * o.dtype.itemsize for o in outs)
    return pl.pallas_call(
        kernel,
        in_specs=resident(len(args)),
        out_specs=resident(len(outs)),
        out_shape=list(outs),
        compiler_params=params(6),
        cost_estimate=cost(count, count),
        name=name,
    )(*args)


def project(heads, weight, resid, gain, bias, deep, side):
    tokens = heads.shape[0]
    features = weight.shape[1]
    rows = tokens // side.size
    own = rows // deep.size
    quarter = features // deep.size
    wide = block_of(features, 1152)
    steps = features // wide

    def kernel(*refs):
        sources, outs = refs[:5], refs[5 : 8 + side.size]
        heads, weight, resid, gain, bias, sems = refs[8 + side.size :]
        packed, gain_row, bias_row, keep, *send = outs
        smalls = [
            pltpu.make_async_copy(source, here, sems.at[i])
            for i, (source, here) in enumerate([(sources[0], heads), *zip(sources[2:], (resid, gain, bias))])
        ]
        blocks = []
        for i in range(steps):
            at = pl.ds(i * wide, wide)
            blocks.append(pltpu.make_async_copy(sources[1].at[:, at], weight.at[:, at], sems.at[4 + i]))
        for copy in smalls[:1] + blocks + smalls[1:]:
            copy.start()

        to = lax.broadcasted_iota(jnp.int32, (tokens, tokens), 0)
        source = lax.broadcasted_iota(jnp.int32, (tokens, tokens), 1)
        across = lax.shift_right_logical(to, rows.bit_length() - 1) ^ side.place()
        down = (lax.shift_right_logical(to, own.bit_length() - 1) & (deep.size - 1)) ^ deep.place()
        wanted = (down * side.size + across) * own + (to & (own - 1))
        pick = jnp.where(source == wanted, 1.0, 0.0).astype(BF16)
        smalls[0].wait()
        turned = jnp.dot(pick, heads[...], preferred_element_type=F32).astype(BF16)
        for i, block in enumerate(blocks):
            block.wait()
            at = slice(i * wide, (i + 1) * wide)
            part = jnp.dot(turned, weight[:, at], preferred_element_type=F32)
            keep[:, at] = part[:rows]
            for k in range(1, side.size):
                send[k - 1][:, at] = part[k * rows : (k + 1) * rows].astype(BF16)
        for copy in smalls[1:]:
            copy.wait()
        values = resid[...].astype(F32)
        pieces = [values[:, q * quarter : (q + 1) * quarter] for q in range(deep.size)]
        packed[...] = jnp.concatenate(pieces, axis=0).astype(BF16)
        gain_row[...] = gain[...].reshape(1, features)
        bias_row[...] = bias[...].reshape(1, features)

    args = (heads, weight, resid, gain, bias)
    return pl.pallas_call(
        kernel,
        in_specs=anywhere(5),
        out_specs=resident(3 + side.size),
        out_shape=[struct((rows, quarter), BF16), struct((1, features), F32), struct((1, features), F32)]
        + [struct((rows, features), F32)]
        + [struct((rows, features), BF16)] * (side.size - 1),
        scratch_shapes=[pltpu.VMEM(x.shape, x.dtype) for x in args] + [pltpu.SemaphoreType.DMA((4 + steps,))],
        compiler_params=params(12),
        cost_estimate=cost(2 * tokens * weight.size, 2 * weight.size),
        name="project",
    )(*[in_hbm(x) for x in args])


def add_up(keep, got, parts, kind, name, beside=None, after=()):
    rows, columns = keep.shape
    part = rows // parts
    extra = [] if beside is None else [beside]
    width = columns + sum(b.shape[1] for b in extra)

    def kernel(*refs):
        ins, outs = refs[: 1 + len(got)], refs[-parts:]
        for p in range(parts):
            at = slice(p * part, (p + 1) * part)
            total = ins[0][at, :]
            for g in ins[1:]:
                total = total + g[at, :].astype(F32)
            outs[p][:, :columns] = total.astype(outs[p].dtype)
        if extra:
            outs[0][:, columns:] = refs[1 + len(got)][...]

    outs = [struct((part, width), kind)] + [struct((part, columns), BF16)] * (parts - 1)
    return small(kernel, outs, keep, *got, *extra, *after, name=name)


def group_sum(parts, own):
    size = len(parts)
    terms = []
    for k, part in enumerate(parts):
        pieces = [part[(j ^ k) * own : ((j ^ k) + 1) * own, :] for j in range(size)]
        terms.append(jnp.concatenate(pieces, axis=0) if size > 1 else part)
    while len(terms) > 1:
        half = len(terms) // 2
        terms = [terms[i] + terms[i + half] for i in range(half)]
    return terms[0]


def residual(parts, gain, after):
    rows = parts[0].shape[0]
    features = gain.shape[1]
    count = len(parts)
    own, quarter = rows // count, features // count

    def kernel(*refs):
        sums, gain, out = refs[:count], refs[count], refs[-1]
        projected = group_sum([p[:, :features].astype(F32) for p in sums], own)
        scale = lax.rsqrt(jnp.mean(projected * projected, axis=-1, keepdims=True) + EPSILON)
        packed = [p[:, features:].astype(F32) for p in sums]
        for q in range(count):
            at = slice(q * quarter, (q + 1) * quarter)
            before = jnp.concatenate([p[q * own : (q + 1) * own, :] for p in packed], axis=0)
            out[:, at] = (before + projected[:, at] * scale * gain[:, at]).astype(BF16)

    return small(kernel, [struct((rows, features), BF16)], *parts, gain, *after, name="residual")[0]


def chunk_at(group, key, width):
    place = 0
    for split, k in zip(group.splits, key):
        place = place * split.size + (split.place() ^ k)
    return pl.multiple_of(place * width, LANES)


def split_columns(keep, got, group, after):
    rows, columns = keep.shape
    width = columns // group.size

    def kernel(*refs):
        ins, outs = refs[: 1 + len(got)], refs[-group.size :]
        for key, out in zip(group.keys, outs):
            at = pl.ds(chunk_at(group, key, width), width)
            total = ins[0][:, at]
            for g in ins[1:]:
                total = total + g[:, at].astype(F32)
            out[...] = total.astype(out.dtype)

    outs = [struct((rows, width), F32)] + [struct((rows, width), BF16)] * (group.size - 1)
    return small(kernel, outs, keep, *got, *after, name="recon")


def fewest(rows):
    return 8 if rows % 8 == 0 else rows


def lay(out, x):
    rows, width = x.shape
    height = out.shape[0]
    for i in range(rows // height):
        out[:, i * width : (i + 1) * width] = x[i * height : (i + 1) * height, :]


def unlaid(x, rows, width):
    height = x.shape[0]
    return jnp.concatenate([x[:, i * width : (i + 1) * width] for i in range(rows // height)], axis=0)


def put_number(out, at, value):
    high = value.astype(BF16)
    low = (value - high.astype(F32)).astype(BF16)
    half = LANES // 2
    out[:, at : at + half] = jnp.broadcast_to(high, (out.shape[0], half))
    out[:, at + half : at + LANES] = jnp.broadcast_to(low, (out.shape[0], half))


def get_number(x, at):
    half = LANES // 2
    return x[:1, at : at + 1].astype(F32) + x[:1, at + half : at + half + 1].astype(F32)


def with_penalty(keep, got, penalties):
    rows, width = keep.shape

    def kernel(*refs):
        ins, numbers, out = refs[: 1 + len(got)], refs[1 + len(got) : -1], refs[-1]
        total = ins[0][...]
        for g in ins[1:]:
            total = total + g[...].astype(F32)
        lay(out, total.astype(BF16))
        penalty = numbers[0][:1, :1]
        for n in numbers[1:]:
            penalty = penalty + n[:1, :1]
        put_number(out, length, penalty)

    height = fewest(rows)
    length = rows // height * width
    return small(kernel, [struct((height, length + LANES), BF16)], keep, *got, *penalties, name="recon")[0]


def tree(terms):
    terms = list(terms)
    while len(terms) > 1:
        half = len(terms) // 2
        terms = [terms[i] + terms[i + half] for i in range(half)]
    return terms[0]


def error_of(parts, resid, bias, group, rows, after):
    height, length = parts[0].shape
    length -= LANES
    width = resid.shape[1] // group.size

    def kernel(*refs):
        sums, resid, bias, out = refs[: len(parts)], refs[len(parts)], refs[len(parts) + 1], refs[-1]
        at = pl.ds(chunk_at(group, group.keys[0], width), width)
        total = unlaid(tree([p[:, :length].astype(F32) for p in sums]), rows, width)
        lay(out, (total + bias[:, at] - resid[:rows, at].astype(F32)).astype(BF16))
        put_number(out, length, tree([get_number(p, length) for p in sums]))

    return small(kernel, [struct((height, length + LANES), BF16)], *parts, resid, bias, *after, name="error")[0]


def stack(pieces, after=()):
    rows, columns = sum(p.shape[0] for p in pieces), pieces[0].shape[1]

    def kernel(*refs):
        row = 0
        for ref in refs[: len(pieces)]:
            refs[-1][row : row + ref.shape[0], :] = ref[...]
            row += ref.shape[0]

    return small(kernel, [struct((rows, columns), pieces[0].dtype)], *pieces, *after, name="stack")[0]


def gather(stages, *pieces):
    pieces = list(pieces)
    for group in reversed(stages):
        if len(pieces) > 4:
            pieces = [stack(pieces)]
        pieces = pieces + [group.swap(p, key) for key in group.keys[1:] for p in pieces]
    return pieces


def copy_rows(source, first, here, sems, start, step=384):
    rows = here.shape[0]
    step = max(b for b in range(16, step + 1, 16) if rows % b == 0)
    return [
        pltpu.make_async_copy(source.at[pl.ds(first + r, step)], here.at[pl.ds(r, step)], sems.at[start + r // step])
        for r in range(0, rows, step)
    ]


MOST_COPIES = 32


def in_order(copies, act):
    def body(_, carry):
        for copy in copies:
            copy.start() if act == "start" else copy.wait()
        return carry

    lax.fori_loop(0, jnp.minimum(lax.axis_index("fsdp") + 1, 1), body, 0)


def load(items, after, name):
    def kernel(*refs):
        sources, results, sems = refs[: len(items)], refs[len(items) + 1 : -1], refs[-1]
        copies = []
        for source, here, (_, first, _) in zip(sources, results, items):
            copies += copy_rows(source, first, here, sems, len(copies))
        for copy in copies:
            copy.start()
        results[-1][...] = jnp.zeros_like(results[-1])
        for copy in copies:
            copy.wait()

    return pl.pallas_call(
        kernel,
        in_specs=anywhere(len(items)) + resident(1),
        out_specs=resident(len(items) + 1),
        out_shape=[pltpu.VMEM((rows, source.shape[1]), source.dtype) for source, _, rows in items]
        + [struct((8, LANES), F32)],
        scratch_shapes=[pltpu.SemaphoreType.DMA((MOST_COPIES,))],
        compiler_params=params(4),
        cost_estimate=cost(0, sum(2 * rows * source.shape[1] for source, _, rows in items)),
        name=name,
    )(*[in_hbm(item[0]) for item in items], after)


def norms(weights, usages, after):
    rows, features = weights.shape
    step = math.gcd(rows, 256)

    def kernel(weight, usage, after, coef, norm_row, penalty):
        total = jnp.zeros((1, 1), F32)
        for r in range(0, rows, step):
            at = slice(r, r + step)
            squares = jnp.zeros((step, LANES), F32)
            for c in range(0, features, LANES):
                w = weight[at, c : c + LANES].astype(F32)
                squares = squares + w * w
            norm = jnp.sqrt(jnp.sum(squares, axis=1, keepdims=True) + EPSILON)
            used = usage[at, :]
            coef[at, :] = SPARSITY * (used / norm)
            norm_row[:, at] = jnp.broadcast_to(norm, (step, LANES)).T[:1, :]
            total = total + jnp.sum(used * norm, axis=0, keepdims=True)
        penalty[...] = jnp.broadcast_to(total, penalty.shape)

    return pl.pallas_call(
        kernel,
        in_specs=resident(3),
        out_specs=resident(3),
        out_shape=[struct((rows, 1), F32), struct((1, rows), F32), struct((8, LANES), F32)],
        compiler_params=params(6),
        cost_estimate=cost(0, 6 * rows * features),
        name="norms",
    )(in_vmem(weights), usages, after)


def encode(parts, held, bias, dec_weight, first, cut, mask_of):
    starts = range(first, dec_weight.shape[0], cut)
    tokens = sum(p.shape[0] for p in parts)
    features = parts[0].shape[1]
    latents = held[0].shape[1]
    wide = block_of(latents, 256)

    def kernel(*refs):
        parts_in, weights = refs[: len(parts)], refs[len(parts) : len(parts) + len(held)]
        bias, source, preact, resid, *here, stacked, sems = refs[len(parts) + len(held) :]
        copies = []
        for start, piece in zip(starts, here):
            copies += copy_rows(source, start, piece, sems, len(copies))
        in_order(copies, "start")
        row = 0
        for part in parts_in:
            stacked[row : row + part.shape[0], :] = part[...]
            row += part.shape[0]
        to = lax.broadcasted_iota(jnp.int32, (tokens, tokens), 0)
        source_row = lax.broadcasted_iota(jnp.int32, (tokens, tokens), 1)
        pick = jnp.where(source_row == (to ^ mask_of()), 1.0, 0.0).astype(BF16)
        block = block_of(features, 512)
        for c in range(0, features, block):
            at = slice(c, c + block)
            resid[:, at] = jnp.dot(pick, stacked[:, at], preferred_element_type=F32).astype(BF16)
        row = bias[...].reshape(1, latents)
        for c in range(0, latents, wide):
            at = slice(c, c + wide)
            total, start = row[:, at], 0
            for w in weights:
                span = w.shape[0]
                total = total + jnp.dot(resid[:, start : start + span], w[:, at], preferred_element_type=F32)
                start += span
            preact[:, at] = total
        in_order(copies, "wait")

    return pl.pallas_call(
        kernel,
        in_specs=resident(len(parts) + len(held) + 1) + anywhere(1),
        out_specs=resident(2 + len(starts)),
        out_shape=[struct((tokens, latents), F32), struct((tokens, features), BF16)]
        + [pltpu.VMEM((cut, features), BF16)] * len(starts),
        scratch_shapes=[pltpu.VMEM((tokens, features), BF16), pltpu.SemaphoreType.DMA((MOST_COPIES,))],
        compiler_params=params(6),
        cost_estimate=cost(2 * tokens * features * latents, 2 * tokens * features),
        name="encode",
    )(*parts, *[in_vmem(w) for w in held], bias, in_hbm(dec_weight))


def decode(preact, held, parts):
    tokens, latents = preact.shape
    features = held[0].shape[1]
    kept = tokens // parts
    sent = max(tokens - kept, 8)
    count = len(held)
    wide = block_of(features, 512)
    sizes = [w.shape[0] for w in held]
    step = math.gcd(*sizes, 256)

    def kernel(preact, *refs):
        weights, keep, send, latents_t = refs[:count], *refs[count : count + 3]
        usages, latents_b = refs[count + 3 : -1], refs[-1]
        for i, (p, r) in enumerate(row_blocks(weights, step)):
            at = slice(i * step, (i + 1) * step)
            value = jnp.maximum(preact[:, at], 0.0)
            latents_b[:, at] = value.astype(BF16)
            turned = value.T
            latents_t[at, :] = turned.astype(BF16)
            usages[p][r : r + step, :] = jnp.sum(turned, axis=1, keepdims=True)
        for c in range(0, features, wide):
            at = slice(c, c + wide)
            part, start = None, 0
            for w, span in zip(weights, sizes):
                term = jnp.dot(latents_b[:, start : start + span], w[:, at], preferred_element_type=F32)
                part = term if part is None else part + term
                start += span
            keep[:, at] = part[:kept]
            if kept < tokens:
                send[:, at] = part[kept:].astype(BF16)

    return pl.pallas_call(
        kernel,
        in_specs=resident(1 + count),
        out_specs=resident(3 + count),
        out_shape=[
            struct((kept, features), F32),
            struct((sent, features), BF16),
            struct((latents, tokens), BF16),
        ]
        + [struct((size, 1), F32) for size in sizes],
        scratch_shapes=[pltpu.VMEM((tokens, latents), BF16)],
        compiler_params=params(6),
        cost_estimate=cost(2 * tokens * features * latents, 6 * tokens * features),
        name="decode",
    )(preact, *[in_vmem(w) for w in held])


def turn(x, after):
    def kernel(x, after, out):
        out[...] = x[...].astype(F32).T.astype(BF16)

    return small(kernel, [struct(x.shape[::-1], BF16)], x, after, name="turn")[0]


def row_blocks(weights, rows):
    return [(p, r) for p, w in enumerate(weights) for r in range(0, w.shape[0], rows)]


def fold(x):
    n = x.shape[0]
    while n > 1 and n % 2 == 0:
        n //= 2
        x = x[:n] + x[n:]
    return x if n == 1 else jnp.sum(x, axis=0, keepdims=True)


def row_blocks(weights, rows):
    return [(p, r) for p, w in enumerate(weights) for r in range(0, w.shape[0], rows)]


def units(refs, height):
    return [ref.at[pl.ds(r, height)] for ref in refs for r in range(0, ref.shape[0], height)]


def assemble(messages, error, width):
    height = messages[0].shape[0]
    groups = error.shape[0] // len(messages) // height
    for i, message in enumerate(messages):
        for g in range(groups):
            at = (i * groups + g) * height
            error[at : at + height, :] = message[:, g * width : (g + 1) * width]


def spans(width):
    wide = min(width, 512)
    return [(c, min(wide, width - c)) for c in range(0, width, wide)]


def outer(latents_t, error, coef, weight):
    return (jnp.dot(latents_t, error, preferred_element_type=F32) + coef * weight.astype(F32)).astype(BF16)


def back_product(error, weight):
    return lax.dot_general(error, weight, (((1,), (1,)), ((), ())), preferred_element_type=F32)


def first_back(parts, height, weights, group):
    features = weights[0].shape[1]
    width = features // group.size
    tokens = sum(p.shape[0] * (p.shape[1] // width) for p in parts)
    latents = sum(w.shape[0] for w in weights)
    rows = math.gcd(*[w.shape[0] for w in weights], 256)

    def kernel(*refs):
        pieces, held = refs[: len(parts)], refs[len(parts) : len(parts) + len(weights)]
        back, error = refs[-2:]
        columns = chunk_at(group, group.keys[0], width)
        assemble(units(pieces, height), error, width)
        for i, (p, r) in enumerate(row_blocks(held, rows)):
            weight = held[p][r : r + rows, pl.ds(columns, width)]
            back[:, i * rows : (i + 1) * rows] = back_product(error[...], weight)

    return pl.pallas_call(
        kernel,
        in_specs=resident(len(parts) + len(weights)),
        out_specs=pl.BlockSpec(memory_space=pltpu.VMEM),
        out_shape=struct((tokens, latents), F32),
        scratch_shapes=[pltpu.VMEM((tokens, width), BF16)],
        compiler_params=params(8),
        cost_estimate=cost(2 * tokens * width * latents, 4 * width * latents),
        name="first_back",
    )(*parts, *[in_vmem(w) for w in weights])


def first_outer(parts, height, latents_t, coefs, weights, group, after):
    latents, tokens = latents_t.shape
    features = weights[0].shape[1]
    width = features // group.size
    count = len(weights)
    rows = math.gcd(*[w.shape[0] for w in weights], 256)

    def kernel(*refs):
        pieces, refs = refs[: len(parts)], refs[len(parts) :]
        coef, held = refs[:count], refs[count : 2 * count]
        latents_t, _, dec_grad, ready, error, stage, sems = refs[2 * count :]
        ready[...] = jnp.zeros_like(ready)
        columns = chunk_at(group, group.keys[0], width)
        assemble(units(pieces, height), error, width)
        copies = []
        for i, (p, r) in enumerate(row_blocks(held, rows)):
            at, inside = slice(i * rows, (i + 1) * rows), slice(r, r + rows)
            for c, wide in spans(width):
                over = pl.ds(pl.multiple_of(columns + c, LANES), wide)
                stage[at, c : c + wide] = outer(
                    latents_t[at, :], error[:, c : c + wide], coef[p][inside, :], held[p][inside, over]
                )
            at = pl.ds(i * rows, rows)
            copies.append(
                pltpu.make_async_copy(stage.at[at], dec_grad.at[at, pl.ds(columns, width)], sems.at[i])
            )
            copies[-1].start()
        for copy in copies:
            copy.wait()

    return pl.pallas_call(
        kernel,
        in_specs=resident(len(parts) + 2 * count + 2),
        out_specs=anywhere(1) + resident(1),
        out_shape=[struct((latents, features), BF16), struct((8, LANES), F32)],
        scratch_shapes=[
            pltpu.VMEM((tokens, width), BF16),
            pltpu.VMEM((latents, width), BF16),
            pltpu.SemaphoreType.DMA((latents // rows,)),
        ],
        compiler_params=params(10),
        cost_estimate=cost(2 * tokens * width * latents, 4 * width * latents),
        name="first_outer",
    )(*parts, *coefs, *[in_vmem(w) for w in weights], latents_t, after)


def gradients(first, others, height, resid_t, preact, latents_t, coefs, weights, norm_rows, dec_grad, back, group):
    tokens, latents = preact.shape
    features = weights[0].shape[1]
    width = features // group.size
    count, size = len(weights), group.size
    pieces = len(first)
    rows = math.gcd(*[w.shape[0] for w in weights], 256)
    span = math.gcd(latents, 512)
    deep = block_of(features, 1152)
    dec_slots, enc_slots = 3, 6
    flat = first + others

    def kernel(*refs):
        chunks = [units(refs[:pieces], height)]
        chunks += [units(refs[pieces : len(flat)], height)[k :: size - 1] for k in range(size - 1)]
        refs = refs[len(flat) :]
        coef, held, norm_row, refs = refs[:count], refs[count : 2 * count], refs[2 * count : 3 * count], refs[3 * count :]
        (resid_t, preact, latents_t, back, _, dec_grad, enc_grad, bias_grad, column_sum, loss,
         error, pulled, sums, dec_stage, enc_stage, dec_sem, enc_sem) = refs
        columns = [chunk_at(group, key, width) for key in group.keys]
        for k in range(size):
            assemble(chunks[k], error.at[k], width)
        where = row_blocks(held, rows)
        dec_copies, enc_copies = [], []

        def products(i):
            p, r = where[i]
            at, inside = slice(i * rows, (i + 1) * rows), slice(r, r + rows)
            total = back[:, at]
            for k in range(1, size):
                for c, wide in spans(width):
                    part = error[k, :, c : c + wide]
                    weight = held[p][inside, pl.ds(pl.multiple_of(columns[k] + c, LANES), wide)]
                    dec_stage[i % dec_slots, k - 1, :, c : c + wide] = outer(
                        latents_t[at, :], part, coef[p][inside, :], weight
                    )
                    total = total + back_product(part, weight)
            total = (total + SPARSITY * norm_row[p][:, inside]) * jax.nn.sigmoid(preact[:, at] / SMOOTHING)
            bias_grad[:, at] = jnp.sum(total, axis=0, keepdims=True)
            pulled[:, at] = total.astype(BF16)

        def send_rows(i):
            slot = i % dec_slots
            for k in range(1, size):
                copy = pltpu.make_async_copy(
                    dec_stage.at[slot, k - 1],
                    dec_grad.at[pl.ds(i * rows, rows), pl.ds(columns[k], width)],
                    dec_sem.at[slot, k - 1],
                )
                copy.start()
                dec_copies.append(copy)

        blocks = [(first, j) for first in range(0, latents, span) for j in range(0, features, deep)]

        def block(n):
            first, j = blocks[n]
            enc_stage[n % enc_slots] = jnp.dot(
                resid_t[j : j + deep, :], pulled[:, first : first + span], preferred_element_type=F32
            ).astype(BF16)

        def send_block(n):
            (first, j), slot = blocks[n], n % enc_slots
            copy = pltpu.make_async_copy(
                enc_stage.at[slot], enc_grad.at[pl.ds(j, deep), pl.ds(first, span)], enc_sem.at[slot]
            )
            copy.start()
            enc_copies.append(copy)

        def free_block(n):
            if n >= enc_slots:
                enc_copies[n - enc_slots].wait()

        each, per = span // rows, features // deep
        done = 0
        for i in range(latents // rows):
            if i >= dec_slots:
                for k in range(1, size):
                    dec_copies[(i - dec_slots) * (size - 1) + k - 1].wait()
            upto = min(done + -(-per // each), i // each * per)
            for n in range(done, upto):
                free_block(n)
            products(i)
            for n in range(done, upto):
                block(n)
            send_rows(i)
            for n in range(done, upto):
                send_block(n)
            done = upto
        for n in range(done, len(blocks)):
            free_block(n)
            block(n)
            send_block(n)

        squares, penalties = [], []
        for k in range(size):
            total = jnp.zeros((1, 1), F32)
            for c, wide in spans(width):
                e = error[k, :, c : c + wide].astype(F32)
                sums[:, pl.ds(pl.multiple_of(columns[k] + c, LANES), wide)] = fold(e)
                total = total + jnp.sum(fold(e * e), axis=1, keepdims=True)
            squares.append(total)
            penalties += [get_number(piece[...], piece.shape[1] - LANES) for piece in chunks[k]]
        column_sum[...] = sums[...].reshape(features)
        value = (0.5 * tree(squares) + SPARSITY * tree(penalties)) / (tokens * features)
        loss[0, 0] = jnp.sum(value)
        for copy in dec_copies[-dec_slots * (size - 1) :] + enc_copies[-enc_slots:]:
            copy.wait()

    return pl.pallas_call(
        kernel,
        in_specs=resident(len(flat) + 3 * count + 4) + anywhere(1),
        out_specs=anywhere(2) + resident(2) + [pl.BlockSpec(memory_space=pltpu.SMEM)],
        out_shape=[
            struct((latents, features), BF16),
            struct((features, latents), BF16),
            struct((1, latents), F32),
            struct((features,), F32),
            struct((1, 1), F32),
        ],
        scratch_shapes=[
            pltpu.VMEM((size, tokens, width), BF16),
            pltpu.VMEM((tokens, latents), BF16),
            pltpu.VMEM((1, features), F32),
            pltpu.VMEM((dec_slots, max(size - 1, 1), rows, width), BF16),
            pltpu.VMEM((enc_slots, deep, span), BF16),
            pltpu.SemaphoreType.DMA((dec_slots, max(size - 1, 1))),
            pltpu.SemaphoreType.DMA((enc_slots,)),
        ],
        input_output_aliases={len(flat) + 3 * count + 4: 0},
        compiler_params=params(18),
        cost_estimate=cost(6 * tokens * features * latents, 4 * features * latents),
        name="gradients",
    )(*flat, *coefs, *[in_vmem(w) for w in weights], *norm_rows, resid_t, preact, latents_t, back, dec_grad)


def make_body(mesh):
    dp, fsdp = mesh.shape["dp"], mesh.shape["fsdp"]
    cores = 2 if dp % 2 == 0 else 1
    depth = 4 if fsdp % 4 == 0 else 1
    core_split, across_split = Split("dp", 1, cores), Split("dp", cores, dp // cores)
    deep_split, side_split = Split("fsdp", fsdp // depth, depth), Split("fsdp", 1, fsdp // depth)
    core, deep, side = Group(mesh, core_split), Group(mesh, deep_split), Group(mesh, side_split)
    if across_split.size * side_split.size <= 4:
        by_token, by_feature = [core], Group(mesh, across_split, side_split)
    else:
        by_token, by_feature = [core, Group(mesh, across_split)], side
    stages = by_token + [by_feature]

    def body(attn_heads, out_proj, resid_pre, post_gain, enc_weight, enc_bias, dec_weight, dec_bias):
        own = resid_pre.shape[0]
        latents, features = dec_weight.shape
        cut = max(latents // 4, LANES)
        depth = features // 3

        def mask():
            place = 0
            for split in (across_split, side_split):
                shared = any(split is s for s in by_feature.splits)
                place = place * split.size + (split.place() if shared else 0)
            return (place * deep_split.size + deep_split.place()) * own

        packed, gain, bias, keep, *send = project(
            attn_heads, out_proj, resid_pre, post_gain, dec_bias, deep_split, side_split
        )
        got = side.swaps(send)
        enc_first, ready = load([(enc_weight, 0, depth)], send[0] if send else keep, "load_first")
        summed = add_up(keep, got, 1, BF16, "heads_y", packed, [ready])[0]
        sums = deep.spread(summed)
        enc_second, enc_third, dec_first, ready = load(
            [(enc_weight, depth, depth), (enc_weight, 2 * depth, depth), (dec_weight, 0, cut)], summed, "load_second"
        )
        resid_own = residual(sums, gain, [ready])
        near = by_feature.spread(resid_own)
        held, ready = [dec_first], []
        if latents == 4 * cut:
            dec_next, *ready = load([(dec_weight, cut, cut)], resid_own, "load_third")
            held.append(dec_next)
        near = near[:1] + [stack(near[1:], ready)] * (len(near) > 1)
        resid_parts = gather(by_token, *near)

        preact, resid_all, *dec_last = encode(
            resid_parts, [enc_first, enc_second, enc_third], enc_bias, dec_weight, cut * len(held), cut, mask
        )
        held += dec_last
        keep, send, latents_t, *used = decode(preact, held, core.size)
        send = [send]
        found = [norms(held[0], used[0], send[0])]
        for i, group in enumerate(by_token):
            got = group.swaps(send)
            if i + 1 < len(by_token):
                keep, *send = add_up(keep, got, by_token[i + 1].size, F32, "recon")
            else:
                keep, *send = split_columns(keep, got, by_feature, found[0][2:])
        got = by_feature.swaps(send)
        found += [norms(w, u, keep) for w, u in zip(held[1:], used[1:])]
        coefs, norm_rows, penalties = [list(x) for x in zip(*found)]
        rows = keep.shape[0]
        keep = with_penalty(keep, got, penalties)
        sums = deep.spread(keep)
        resid_t = turn(resid_all, keep)
        error_own = error_of(sums, resid_all, bias, by_feature, rows, [resid_t])

        others = by_feature.spread(error_own)[1:]
        first, height = gather(by_token, error_own), error_own.shape[0]
        back = first_back(first, height, held, by_feature)
        dec_grad, ready = first_outer(first, height, latents_t, coefs, held, by_feature, back)
        others = gather(by_token, stack(others, [ready])) if others else []
        dec_grad, enc_grad, bias_grad, column_sum, loss = gradients(
            first, others, height, resid_t, preact, latents_t, coefs, held, norm_rows, dec_grad, back, by_feature
        )
        return (enc_grad, bias_grad.reshape(-1), dec_grad, column_sum, loss.reshape(()))

    return body


def solution(mesh):
    placed = (
        P("dp", "fsdp"),
        P("fsdp", None),
        P(("dp", "fsdp"), None),
        P(),
        P(None, ("dp", "fsdp")),
        P(("dp", "fsdp")),
        P(("dp", "fsdp"), None),
        P(),
    )
    return jax.shard_map(
        make_body(mesh),
        mesh=mesh,
        in_specs=placed,
        out_specs=(P(None, ("dp", "fsdp")), P(("dp", "fsdp")), P(("dp", "fsdp"), None), P(), P()),
        check_vma=False,
    )
```

```python
import functools
import itertools
import math

import jax
import jax.numpy as jnp
from jax import lax
from jax.experimental import pallas as pl
from jax.experimental.pallas import tpu as pltpu
from jax.sharding import PartitionSpec as P

SPARSITY = 0.25
SMOOTHING = 0.1
EPSILON = 1e-06
F32 = jnp.float32
BF16 = jnp.bfloat16
LANES = 128


class Split:
    def __init__(self, axis, inner, size):
        self.axis, self.inner, self.size = axis, inner, size

    def place(self):
        return (lax.axis_index(self.axis) // self.inner) % self.size


class Group:
    def __init__(self, mesh, *splits):
        self.lengths = {axis: mesh.shape[axis] for axis in ("dp", "fsdp")}
        self.splits = splits
        self.size = math.prod(s.size for s in splits)
        self.keys = list(itertools.product(*(range(s.size) for s in splits)))

    def swap(self, x, key):
        pairs = []
        for d in range(self.lengths["dp"]):
            for f in range(self.lengths["fsdp"]):
                to = {"dp": d, "fsdp": f}
                for split, k in zip(self.splits, key):
                    a = (to[split.axis] // split.inner) % split.size
                    to[split.axis] += ((a ^ k) - a) * split.inner
                width = self.lengths["fsdp"]
                pairs.append((d * width + f, to["dp"] * width + to["fsdp"]))
        return lax.ppermute(x, ("dp", "fsdp"), pairs)

    def swaps(self, pieces):
        return [self.swap(p, key) for p, key in zip(pieces, self.keys[1:])]

    def spread(self, x):
        return [x] + [self.swap(x, key) for key in self.keys[1:]]


def block_of(total, most):
    return max(b for b in range(LANES, most + 1, LANES) if total % b == 0)


def resident(count):
    return [pl.BlockSpec(memory_space=pltpu.VMEM)] * count


def anywhere(count):
    return [pl.BlockSpec(memory_space=pl.ANY)] * count


def in_hbm(x):
    return pltpu.with_memory_space_constraint(x, pltpu.HBM)


def in_vmem(x):
    return pltpu.with_memory_space_constraint(x, pltpu.VMEM)


def params(megabytes):
    return pltpu.CompilerParams(vmem_limit_bytes=megabytes * 1024 * 1024)


def cost(flops, count):
    return pl.CostEstimate(flops=flops, bytes_accessed=count, transcendentals=0)


def struct(shape, kind):
    return jax.ShapeDtypeStruct(shape, kind)


def small(kernel, outs, *args, name):
    count = sum(x.size * x.dtype.itemsize for x in args) + sum(o.size * o.dtype.itemsize for o in outs)
    return pl.pallas_call(
        kernel,
        in_specs=resident(len(args)),
        out_specs=resident(len(outs)),
        out_shape=list(outs),
        compiler_params=params(6),
        cost_estimate=cost(count, count),
        name=name,
    )(*args)


def project(heads, weight, resid, gain, bias, deep, side):
    tokens = heads.shape[0]
    features = weight.shape[1]
    rows = tokens // side.size
    own = rows // deep.size
    quarter = features // deep.size
    wide = block_of(features, 1152)
    steps = features // wide

    def kernel(*refs):
        sources, outs = refs[:5], refs[5 : 8 + side.size]
        heads, weight, resid, gain, bias, sems = refs[8 + side.size :]
        packed, gain_row, bias_row, keep, *send = outs
        smalls = [
            pltpu.make_async_copy(source, here, sems.at[i])
            for i, (source, here) in enumerate([(sources[0], heads), *zip(sources[2:], (resid, gain, bias))])
        ]
        blocks = []
        for i in range(steps):
            at = pl.ds(i * wide, wide)
            blocks.append(pltpu.make_async_copy(sources[1].at[:, at], weight.at[:, at], sems.at[4 + i]))
        for copy in smalls[:1] + blocks + smalls[1:]:
            copy.start()

        to = lax.broadcasted_iota(jnp.int32, (tokens, tokens), 0)
        source = lax.broadcasted_iota(jnp.int32, (tokens, tokens), 1)
        across = lax.shift_right_logical(to, rows.bit_length() - 1) ^ side.place()
        down = (lax.shift_right_logical(to, own.bit_length() - 1) & (deep.size - 1)) ^ deep.place()
        wanted = (down * side.size + across) * own + (to & (own - 1))
        pick = jnp.where(source == wanted, 1.0, 0.0).astype(BF16)
        smalls[0].wait()
        turned = jnp.dot(pick, heads[...], preferred_element_type=F32).astype(BF16)
        for i, block in enumerate(blocks):
            block.wait()
            at = slice(i * wide, (i + 1) * wide)
            part = jnp.dot(turned, weight[:, at], preferred_element_type=F32)
            keep[:, at] = part[:rows]
            for k in range(1, side.size):
                send[k - 1][:, at] = part[k * rows : (k + 1) * rows].astype(BF16)
        for copy in smalls[1:]:
            copy.wait()
        values = resid[...].astype(F32)
        pieces = [values[:, q * quarter : (q + 1) * quarter] for q in range(deep.size)]
        packed[...] = jnp.concatenate(pieces, axis=0).astype(BF16)
        gain_row[...] = gain[...].reshape(1, features)
        bias_row[...] = bias[...].reshape(1, features)

    args = (heads, weight, resid, gain, bias)
    return pl.pallas_call(
        kernel,
        in_specs=anywhere(5),
        out_specs=resident(3 + side.size),
        out_shape=[struct((rows, quarter), BF16), struct((1, features), F32), struct((1, features), F32)]
        + [struct((rows, features), F32)]
        + [struct((rows, features), BF16)] * (side.size - 1),
        scratch_shapes=[pltpu.VMEM(x.shape, x.dtype) for x in args] + [pltpu.SemaphoreType.DMA((4 + steps,))],
        compiler_params=params(12),
        cost_estimate=cost(2 * tokens * weight.size, 2 * weight.size),
        name="project",
    )(*[in_hbm(x) for x in args])


def add_up(keep, got, parts, kind, name, beside=None, after=()):
    rows, columns = keep.shape
    part = rows // parts
    extra = [] if beside is None else [beside]
    width = columns + sum(b.shape[1] for b in extra)

    def kernel(*refs):
        ins, outs = refs[: 1 + len(got)], refs[-parts:]
        for p in range(parts):
            at = slice(p * part, (p + 1) * part)
            total = ins[0][at, :]
            for g in ins[1:]:
                total = total + g[at, :].astype(F32)
            outs[p][:, :columns] = total.astype(outs[p].dtype)
        if extra:
            outs[0][:, columns:] = refs[1 + len(got)][...]

    outs = [struct((part, width), kind)] + [struct((part, columns), BF16)] * (parts - 1)
    return small(kernel, outs, keep, *got, *extra, *after, name=name)


def group_sum(parts, own):
    size = len(parts)
    terms = []
    for k, part in enumerate(parts):
        pieces = [part[(j ^ k) * own : ((j ^ k) + 1) * own, :] for j in range(size)]
        terms.append(jnp.concatenate(pieces, axis=0) if size > 1 else part)
    while len(terms) > 1:
        half = len(terms) // 2
        terms = [terms[i] + terms[i + half] for i in range(half)]
    return terms[0]


def residual(parts, gain, after):
    rows = parts[0].shape[0]
    features = gain.shape[1]
    count = len(parts)
    own, quarter = rows // count, features // count
    parts, places = in_turn(parts)

    def kernel(*refs):
        sums, gain, out = [refs[i] for i in places], refs[count], refs[-1]
        projected = group_sum([p[:, :features].astype(F32) for p in sums], own)
        scale = lax.rsqrt(jnp.mean(projected * projected, axis=-1, keepdims=True) + EPSILON)
        packed = [p[:, features:].astype(F32) for p in sums]
        for q in range(count):
            at = slice(q * quarter, (q + 1) * quarter)
            before = jnp.concatenate([p[q * own : (q + 1) * own, :] for p in packed], axis=0)
            out[:, at] = (before + projected[:, at] * scale * gain[:, at]).astype(BF16)

    return small(kernel, [struct((rows, features), BF16)], *parts, gain, *after, name="residual")[0]


def chunk_at(group, key, width):
    place = 0
    for split, k in zip(group.splits, key):
        place = place * split.size + (split.place() ^ k)
    return pl.multiple_of(place * width, LANES)


def split_columns(keep, got, group, after):
    rows, columns = keep.shape
    width = columns // group.size

    def kernel(*refs):
        ins, outs = refs[: 1 + len(got)], refs[-group.size :]
        for key, out in zip(group.keys, outs):
            at = pl.ds(chunk_at(group, key, width), width)
            total = ins[0][:, at]
            for g in ins[1:]:
                total = total + g[:, at].astype(F32)
            out[...] = total.astype(out.dtype)

    outs = [struct((rows, width), F32)] + [struct((rows, width), BF16)] * (group.size - 1)
    return small(kernel, outs, keep, *got, *after, name="recon")


def fewest(rows):
    return 8 if rows % 8 == 0 else rows


def lay(out, x):
    rows, width = x.shape
    height = out.shape[0]
    for i in range(rows // height):
        out[:, i * width : (i + 1) * width] = x[i * height : (i + 1) * height, :]


def unlaid(x, rows, width):
    height = x.shape[0]
    return jnp.concatenate([x[:, i * width : (i + 1) * width] for i in range(rows // height)], axis=0)


def put_number(out, at, value):
    high = value.astype(BF16)
    low = (value - high.astype(F32)).astype(BF16)
    half = LANES // 2
    out[:, at : at + half] = jnp.broadcast_to(high, (out.shape[0], half))
    out[:, at + half : at + LANES] = jnp.broadcast_to(low, (out.shape[0], half))


def get_number(x, at):
    half = LANES // 2
    return x[:1, at : at + 1].astype(F32) + x[:1, at + half : at + half + 1].astype(F32)


def with_penalty(keep, got, penalties):
    rows, width = keep.shape

    def kernel(*refs):
        ins, numbers, out = refs[: 1 + len(got)], refs[1 + len(got) : -1], refs[-1]
        total = ins[0][...]
        for g in ins[1:]:
            total = total + g[...].astype(F32)
        lay(out, total.astype(BF16))
        penalty = numbers[0][:1, :1]
        for n in numbers[1:]:
            penalty = penalty + n[:1, :1]
        put_number(out, length, penalty)

    height = fewest(rows)
    length = rows // height * width
    return small(kernel, [struct((height, length + LANES), BF16)], keep, *got, *penalties, name="recon")[0]


def tree(terms):
    terms = list(terms)
    while len(terms) > 1:
        half = len(terms) // 2
        terms = [terms[i] + terms[i + half] for i in range(half)]
    return terms[0]


def in_turn(parts):
    order = [0, 1, 3, 2] if len(parts) == 4 else list(range(len(parts)))
    return [parts[i] for i in order], [order.index(i) for i in range(len(parts))]


def error_of(parts, resid, bias, group, rows, after):
    parts, places = in_turn(parts)
    height, length = parts[0].shape
    length -= LANES
    width = resid.shape[1] // group.size

    def kernel(*refs):
        sums, resid, bias, out = refs[: len(parts)], refs[len(parts)], refs[len(parts) + 1], refs[-1]
        at = pl.ds(chunk_at(group, group.keys[0], width), width)
        sums = [sums[i] for i in places]
        total = unlaid(tree([p[:, :length].astype(F32) for p in sums]), rows, width)
        lay(out, (total + bias[:, at] - resid[:rows, at].astype(F32)).astype(BF16))
        put_number(out, length, tree([get_number(p, length) for p in sums]))

    return small(kernel, [struct((height, length + LANES), BF16)], *parts, resid, bias, *after, name="error")[0]


def stack(pieces, after=()):
    rows, columns = sum(p.shape[0] for p in pieces), pieces[0].shape[1]

    def kernel(*refs):
        row = 0
        for ref in refs[: len(pieces)]:
            refs[-1][row : row + ref.shape[0], :] = ref[...]
            row += ref.shape[0]

    return small(kernel, [struct((rows, columns), pieces[0].dtype)], *pieces, *after, name="stack")[0]


def gather(stages, *pieces):
    pieces = list(pieces)
    for group in reversed(stages):
        if len(pieces) > 4:
            pieces = [stack(pieces)]
        pieces = pieces + [group.swap(p, key) for key in group.keys[1:] for p in pieces]
    return pieces


def copy_rows(source, first, here, sems, start, step=384):
    rows = here.shape[0]
    step = max(b for b in range(16, step + 1, 16) if rows % b == 0)
    return [
        pltpu.make_async_copy(source.at[pl.ds(first + r, step)], here.at[pl.ds(r, step)], sems.at[start + r // step])
        for r in range(0, rows, step)
    ]


MOST_COPIES = 32


def in_order(copies, act):
    def body(_, carry):
        for copy in copies:
            copy.start() if act == "start" else copy.wait()
        return carry

    lax.fori_loop(0, jnp.minimum(lax.axis_index("fsdp") + 1, 1), body, 0)


def load(items, after, name):
    def kernel(*refs):
        sources, results, sems = refs[: len(items)], refs[len(items) + 1 : -1], refs[-1]
        copies = []
        for source, here, (_, first, _) in zip(sources, results, items):
            copies += copy_rows(source, first, here, sems, len(copies))
        for copy in copies:
            copy.start()
        results[-1][...] = jnp.zeros_like(results[-1])
        for copy in copies:
            copy.wait()

    return pl.pallas_call(
        kernel,
        in_specs=anywhere(len(items)) + resident(1),
        out_specs=resident(len(items) + 1),
        out_shape=[pltpu.VMEM((rows, source.shape[1]), source.dtype) for source, _, rows in items]
        + [struct((8, LANES), F32)],
        scratch_shapes=[pltpu.SemaphoreType.DMA((MOST_COPIES,))],
        compiler_params=params(4),
        cost_estimate=cost(0, sum(2 * rows * source.shape[1] for source, _, rows in items)),
        name=name,
    )(*[in_hbm(item[0]) for item in items], after)


def norms(weights, usages, after):
    rows, features = weights.shape
    step = math.gcd(rows, 256)

    def kernel(weight, usage, after, coef, norm_row, penalty):
        total = jnp.zeros((1, 1), F32)
        for r in range(0, rows, step):
            at = slice(r, r + step)
            squares = jnp.zeros((step, LANES), F32)
            for c in range(0, features, LANES):
                w = weight[at, c : c + LANES].astype(F32)
                squares = squares + w * w
            norm = jnp.sqrt(jnp.sum(squares, axis=1, keepdims=True) + EPSILON)
            used = usage[at, :]
            coef[at, :] = SPARSITY * (used / norm)
            norm_row[:, at] = jnp.broadcast_to(norm, (step, LANES)).T[:1, :]
            total = total + jnp.sum(used * norm, axis=0, keepdims=True)
        penalty[...] = jnp.broadcast_to(total, penalty.shape)

    return pl.pallas_call(
        kernel,
        in_specs=resident(3),
        out_specs=resident(3),
        out_shape=[struct((rows, 1), F32), struct((1, rows), F32), struct((8, LANES), F32)],
        compiler_params=params(6),
        cost_estimate=cost(0, 6 * rows * features),
        name="norms",
    )(in_vmem(weights), usages, after)


def encode(parts, held, bias, dec_weight, first, cut, mask_of):
    starts = range(first, dec_weight.shape[0], cut)
    tokens = sum(p.shape[0] for p in parts)
    features = parts[0].shape[1]
    latents = held[0].shape[1]
    wide = block_of(latents, 256)

    def kernel(*refs):
        parts_in, weights = refs[: len(parts)], refs[len(parts) : len(parts) + len(held)]
        bias, source, preact, resid, *here, stacked, sems = refs[len(parts) + len(held) :]
        copies = []
        for start, piece in zip(starts, here):
            copies += copy_rows(source, start, piece, sems, len(copies))
        in_order(copies, "start")
        row = 0
        for part in parts_in:
            stacked[row : row + part.shape[0], :] = part[...]
            row += part.shape[0]
        to = lax.broadcasted_iota(jnp.int32, (tokens, tokens), 0)
        source_row = lax.broadcasted_iota(jnp.int32, (tokens, tokens), 1)
        pick = jnp.where(source_row == (to ^ mask_of()), 1.0, 0.0).astype(BF16)
        block = block_of(features, 512)
        for c in range(0, features, block):
            at = slice(c, c + block)
            resid[:, at] = jnp.dot(pick, stacked[:, at], preferred_element_type=F32).astype(BF16)
        row = bias[...].reshape(1, latents)
        for c in range(0, latents, wide):
            at = slice(c, c + wide)
            total, start = row[:, at], 0
            for w in weights:
                span = w.shape[0]
                total = total + jnp.dot(resid[:, start : start + span], w[:, at], preferred_element_type=F32)
                start += span
            preact[:, at] = total
        in_order(copies, "wait")

    return pl.pallas_call(
        kernel,
        in_specs=resident(len(parts) + len(held) + 1) + anywhere(1),
        out_specs=resident(2 + len(starts)),
        out_shape=[struct((tokens, latents), F32), struct((tokens, features), BF16)]
        + [pltpu.VMEM((cut, features), BF16)] * len(starts),
        scratch_shapes=[pltpu.VMEM((tokens, features), BF16), pltpu.SemaphoreType.DMA((MOST_COPIES,))],
        compiler_params=params(6),
        cost_estimate=cost(2 * tokens * features * latents, 2 * tokens * features),
        name="encode",
    )(*parts, *[in_vmem(w) for w in held], bias, in_hbm(dec_weight))


def decode(preact, held, parts):
    tokens, latents = preact.shape
    features = held[0].shape[1]
    kept = tokens // parts
    sent = max(tokens - kept, 8)
    count = len(held)
    wide = block_of(features, 512)
    sizes = [w.shape[0] for w in held]
    step = math.gcd(*sizes, 256)

    def kernel(preact, *refs):
        weights, keep, send, latents_t = refs[:count], *refs[count : count + 3]
        usages, latents_b = refs[count + 3 : -1], refs[-1]
        for i, (p, r) in enumerate(row_blocks(weights, step)):
            at = slice(i * step, (i + 1) * step)
            value = jnp.maximum(preact[:, at], 0.0)
            latents_b[:, at] = value.astype(BF16)
            turned = value.T
            latents_t[at, :] = turned.astype(BF16)
            usages[p][r : r + step, :] = jnp.sum(turned, axis=1, keepdims=True)
        for c in range(0, features, wide):
            at = slice(c, c + wide)
            part, start = None, 0
            for w, span in zip(weights, sizes):
                term = jnp.dot(latents_b[:, start : start + span], w[:, at], preferred_element_type=F32)
                part = term if part is None else part + term
                start += span
            keep[:, at] = part[:kept]
            if kept < tokens:
                send[:, at] = part[kept:].astype(BF16)

    return pl.pallas_call(
        kernel,
        in_specs=resident(1 + count),
        out_specs=resident(3 + count),
        out_shape=[
            struct((kept, features), F32),
            struct((sent, features), BF16),
            struct((latents, tokens), BF16),
        ]
        + [struct((size, 1), F32) for size in sizes],
        scratch_shapes=[pltpu.VMEM((tokens, latents), BF16)],
        compiler_params=params(6),
        cost_estimate=cost(2 * tokens * features * latents, 6 * tokens * features),
        name="decode",
    )(preact, *[in_vmem(w) for w in held])


def turn(x, after):
    def kernel(x, after, out):
        out[...] = x[...].astype(F32).T.astype(BF16)

    return small(kernel, [struct(x.shape[::-1], BF16)], x, after, name="turn")[0]


def row_blocks(weights, rows):
    return [(p, r) for p, w in enumerate(weights) for r in range(0, w.shape[0], rows)]


def fold(x):
    n = x.shape[0]
    while n > 1 and n % 2 == 0:
        n //= 2
        x = x[:n] + x[n:]
    return x if n == 1 else jnp.sum(x, axis=0, keepdims=True)


def row_blocks(weights, rows):
    return [(p, r) for p, w in enumerate(weights) for r in range(0, w.shape[0], rows)]


def units(refs, height):
    return [ref.at[pl.ds(r, height)] for ref in refs for r in range(0, ref.shape[0], height)]


def assemble(messages, error, width):
    height = messages[0].shape[0]
    groups = error.shape[0] // len(messages) // height
    for i, message in enumerate(messages):
        for g in range(groups):
            at = (i * groups + g) * height
            error[at : at + height, :] = message[:, g * width : (g + 1) * width]


def spans(width):
    wide = min(width, 512)
    return [(c, min(wide, width - c)) for c in range(0, width, wide)]


def whole_tiles(width):
    return width // 256 * 256


def outer(latents_t, error, coef, weight):
    return (jnp.dot(latents_t, error, preferred_element_type=F32) + coef * weight.astype(F32)).astype(BF16)


def back_product(error, weight):
    return lax.dot_general(error, weight, (((1,), (1,)), ((), ())), preferred_element_type=F32)


def first_back(parts, height, weights, group):
    features = weights[0].shape[1]
    width = features // group.size
    tokens = sum(p.shape[0] * (p.shape[1] // width) for p in parts)
    latents = sum(w.shape[0] for w in weights)
    rows = math.gcd(*[w.shape[0] for w in weights], 256)

    def kernel(*refs):
        pieces, held = refs[: len(parts)], refs[len(parts) : len(parts) + len(weights)]
        back, error = refs[-2:]
        columns = chunk_at(group, group.keys[0], width)
        assemble(units(pieces, height), error, width)
        for i, (p, r) in enumerate(row_blocks(held, rows)):
            weight = held[p][r : r + rows, pl.ds(columns, width)]
            back[:, i * rows : (i + 1) * rows] = back_product(error[...], weight)

    return pl.pallas_call(
        kernel,
        in_specs=resident(len(parts) + len(weights)),
        out_specs=pl.BlockSpec(memory_space=pltpu.VMEM),
        out_shape=struct((tokens, latents), F32),
        scratch_shapes=[pltpu.VMEM((tokens, width), BF16)],
        compiler_params=params(8),
        cost_estimate=cost(2 * tokens * width * latents, 4 * width * latents),
        name="first_back",
    )(*parts, *[in_vmem(w) for w in weights])


def first_outer(parts, height, latents_t, coefs, weights, group, after):
    latents, tokens = latents_t.shape
    features = weights[0].shape[1]
    width = features // group.size
    count = len(weights)
    rows = math.gcd(*[w.shape[0] for w in weights], 256)

    def kernel(*refs):
        pieces, refs = refs[: len(parts)], refs[len(parts) :]
        coef, held = refs[:count], refs[count : 2 * count]
        latents_t, _, dec_grad, ready, error, stage, sems = refs[2 * count :]
        ready[...] = jnp.zeros_like(ready)
        columns = chunk_at(group, group.keys[0], width)
        assemble(units(pieces, height), error, width)
        copies = []
        for i, (p, r) in enumerate(row_blocks(held, rows)):
            at, inside = slice(i * rows, (i + 1) * rows), slice(r, r + rows)
            for c, wide in spans(width):
                over = pl.ds(pl.multiple_of(columns + c, LANES), wide)
                stage[at, c : c + wide] = outer(
                    latents_t[at, :], error[:, c : c + wide], coef[p][inside, :], held[p][inside, over]
                )
            at = pl.ds(i * rows, rows)
            copies.append(
                pltpu.make_async_copy(stage.at[at], dec_grad.at[at, pl.ds(columns, width)], sems.at[i])
            )
            copies[-1].start()
        for copy in copies:
            copy.wait()

    return pl.pallas_call(
        kernel,
        in_specs=resident(len(parts) + 2 * count + 2),
        out_specs=anywhere(1) + resident(1),
        out_shape=[struct((latents, features), BF16), struct((8, LANES), F32)],
        scratch_shapes=[
            pltpu.VMEM((tokens, width), BF16),
            pltpu.VMEM((latents, width), BF16),
            pltpu.SemaphoreType.DMA((latents // rows,)),
        ],
        compiler_params=params(10),
        cost_estimate=cost(2 * tokens * width * latents, 4 * width * latents),
        name="first_outer",
    )(*parts, *coefs, *[in_vmem(w) for w in weights], latents_t, after)


def gradients(first, others, height, resid_t, preact, latents_t, coefs, weights, norm_rows, dec_grad, back, group):
    tokens, latents = preact.shape
    features = weights[0].shape[1]
    width = features // group.size
    count, size = len(weights), group.size
    pieces = len(first)
    rows = math.gcd(*[w.shape[0] for w in weights], 256)
    span = math.gcd(latents, 512)
    deep = block_of(features, 1152)
    dec_slots, enc_slots = 3, 6
    main = whole_tiles(width)
    half = math.gcd(span, 256)
    flat = first + others

    def kernel(*refs):
        chunks = [units(refs[:pieces], height)]
        chunks += [units(refs[pieces : len(flat)], height)[k :: size - 1] for k in range(size - 1)]
        refs = refs[len(flat) :]
        coef, held, norm_row, refs = refs[:count], refs[count : 2 * count], refs[2 * count : 3 * count], refs[3 * count :]
        (resid_t, preact, latents_t, back, _, dec_grad, enc_grad, bias_grad, column_sum, loss,
         error, ends, pulled, sums, dec_stage, enc_stage, dec_sem, enc_sem) = refs
        columns = [chunk_at(group, key, width) for key in group.keys]
        for k in range(size):
            assemble(chunks[k], error.at[k], width)
        for k in range(1, size):
            if main < width:
                ends[:, (k - 1) * (width - main) : k * (width - main)] = error[k, :, main:]
        where = row_blocks(held, rows)
        dec_copies, enc_copies = [], []

        def products(i):
            p, r = where[i]
            at, inside = slice(i * rows, (i + 1) * rows), slice(r, r + rows)
            total = back[:, at]
            for k in range(1, size):
                for c, wide in spans(main):
                    part = error[k, :, c : c + wide]
                    weight = held[p][inside, pl.ds(pl.multiple_of(columns[k] + c, LANES), wide)]
                    dec_stage[i % dec_slots, k - 1, :, c : c + wide] = outer(
                        latents_t[at, :], part, coef[p][inside, :], weight
                    )
                    total = total + back_product(part, weight)
            if main < width and size > 1:
                weight = jnp.concatenate(
                    [
                        held[p][inside, pl.ds(pl.multiple_of(columns[k] + main, LANES), width - main)]
                        for k in range(1, size)
                    ],
                    axis=1,
                )
                product = outer(latents_t[at, :], ends[...], coef[p][inside, :], weight)
                for k in range(1, size):
                    over = slice((k - 1) * (width - main), k * (width - main))
                    dec_stage[i % dec_slots, k - 1, :, main:] = product[:, over]
                total = total + back_product(ends[...], weight)
            total = (total + SPARSITY * norm_row[p][:, inside]) * jax.nn.sigmoid(preact[:, at] / SMOOTHING)
            bias_grad[:, at] = jnp.sum(total, axis=0, keepdims=True)
            pulled[:, at] = total.astype(BF16)

        def send_rows(i):
            slot = i % dec_slots
            for k in range(1, size):
                copy = pltpu.make_async_copy(
                    dec_stage.at[slot, k - 1],
                    dec_grad.at[pl.ds(i * rows, rows), pl.ds(columns[k], width)],
                    dec_sem.at[slot, k - 1],
                )
                copy.start()
                dec_copies.append(copy)

        blocks = [(first, j) for first in range(0, latents, span) for j in range(0, features, deep)]

        def block(n):
            first, j = blocks[n]
            part = block_of(deep, 384)
            for r in range(0, deep, part):
                for c in range(0, span, half):
                    enc_stage[n % enc_slots, r : r + part, c : c + half] = jnp.dot(
                        resid_t[j + r : j + r + part, :],
                        pulled[:, first + c : first + c + half],
                        preferred_element_type=F32,
                    ).astype(BF16)

        def send_block(n):
            (first, j), slot = blocks[n], n % enc_slots
            copy = pltpu.make_async_copy(
                enc_stage.at[slot], enc_grad.at[pl.ds(j, deep), pl.ds(first, span)], enc_sem.at[slot]
            )
            copy.start()
            enc_copies.append(copy)

        def free_block(n):
            if n >= enc_slots:
                enc_copies[n - enc_slots].wait()

        each, per = span // rows, features // deep
        done = 0
        for i in range(latents // rows):
            if i >= dec_slots:
                for k in range(1, size):
                    dec_copies[(i - dec_slots) * (size - 1) + k - 1].wait()
            upto = min(done + -(-per // each), i // each * per)
            for n in range(done, upto):
                free_block(n)
            products(i)
            for n in range(done, upto):
                block(n)
            send_rows(i)
            for n in range(done, upto):
                send_block(n)
            done = upto
        for n in range(done, len(blocks)):
            free_block(n)
            block(n)
            send_block(n)

        squares, penalties = [], []
        for k in range(size):
            total = jnp.zeros((1, 1), F32)
            for c, wide in spans(width):
                e = error[k, :, c : c + wide].astype(F32)
                sums[:, pl.ds(pl.multiple_of(columns[k] + c, LANES), wide)] = fold(e)
                total = total + jnp.sum(fold(e * e), axis=1, keepdims=True)
            squares.append(total)
            penalties += [get_number(piece[...], piece.shape[1] - LANES) for piece in chunks[k]]
        column_sum[...] = sums[...].reshape(features)
        value = (0.5 * tree(squares) + SPARSITY * tree(penalties)) / (tokens * features)
        loss[0, 0] = jnp.sum(value)
        for copy in dec_copies[-dec_slots * (size - 1) :] + enc_copies[-enc_slots:]:
            copy.wait()

    return pl.pallas_call(
        kernel,
        in_specs=resident(len(flat) + 3 * count + 4) + anywhere(1),
        out_specs=anywhere(2) + resident(2) + [pl.BlockSpec(memory_space=pltpu.SMEM)],
        out_shape=[
            struct((latents, features), BF16),
            struct((features, latents), BF16),
            struct((1, latents), F32),
            struct((features,), F32),
            struct((1, 1), F32),
        ],
        scratch_shapes=[
            pltpu.VMEM((size, tokens, width), BF16),
            pltpu.VMEM((tokens, max(size - 1, 1) * max(width - main, LANES)), BF16),
            pltpu.VMEM((tokens, latents), BF16),
            pltpu.VMEM((1, features), F32),
            pltpu.VMEM((dec_slots, max(size - 1, 1), rows, width), BF16),
            pltpu.VMEM((enc_slots, deep, span), BF16),
            pltpu.SemaphoreType.DMA((dec_slots, max(size - 1, 1))),
            pltpu.SemaphoreType.DMA((enc_slots,)),
        ],
        input_output_aliases={len(flat) + 3 * count + 4: 0},
        compiler_params=params(18),
        cost_estimate=cost(6 * tokens * features * latents, 4 * features * latents),
        name="gradients",
    )(*flat, *coefs, *[in_vmem(w) for w in weights], *norm_rows, resid_t, preact, latents_t, back, dec_grad)


def make_body(mesh):
    dp, fsdp = mesh.shape["dp"], mesh.shape["fsdp"]
    cores = 2 if dp % 2 == 0 else 1
    depth = 4 if fsdp % 4 == 0 else 1
    core_split, across_split = Split("dp", 1, cores), Split("dp", cores, dp // cores)
    deep_split, side_split = Split("fsdp", fsdp // depth, depth), Split("fsdp", 1, fsdp // depth)
    core, deep, side = Group(mesh, core_split), Group(mesh, deep_split), Group(mesh, side_split)
    if across_split.size * side_split.size <= 4:
        by_token, by_feature = [core], Group(mesh, across_split, side_split)
    else:
        by_token, by_feature = [core, Group(mesh, across_split)], side
    stages = by_token + [by_feature]

    def body(attn_heads, out_proj, resid_pre, post_gain, enc_weight, enc_bias, dec_weight, dec_bias):
        own = resid_pre.shape[0]
        latents, features = dec_weight.shape
        cut = max(latents // 4, LANES)
        depth = features // 3

        def mask():
            place = 0
            for split in (across_split, side_split):
                shared = any(split is s for s in by_feature.splits)
                place = place * split.size + (split.place() if shared else 0)
            return (place * deep_split.size + deep_split.place()) * own

        packed, gain, bias, keep, *send = project(
            attn_heads, out_proj, resid_pre, post_gain, dec_bias, deep_split, side_split
        )
        got = side.swaps(send)
        enc_first, ready = load([(enc_weight, 0, depth)], send[0] if send else keep, "load_first")
        summed = add_up(keep, got, 1, BF16, "heads_y", packed, [ready])[0]
        sums = deep.spread(summed)
        enc_second, enc_third, dec_first, ready = load(
            [(enc_weight, depth, depth), (enc_weight, 2 * depth, depth), (dec_weight, 0, cut)], summed, "load_second"
        )
        resid_own = residual(sums, gain, [ready])
        near = by_feature.spread(resid_own)
        held, ready = [dec_first], []
        if latents == 4 * cut:
            dec_next, *ready = load([(dec_weight, cut, cut)], resid_own, "load_third")
            held.append(dec_next)
        near = near[:1] + [stack(near[1:], ready)] * (len(near) > 1)
        resid_parts = gather(by_token, *near)

        preact, resid_all, *dec_last = encode(
            resid_parts, [enc_first, enc_second, enc_third], enc_bias, dec_weight, cut * len(held), cut, mask
        )
        held += dec_last
        keep, send, latents_t, *used = decode(preact, held, core.size)
        send = [send]
        found = [norms(held[0], used[0], send[0])]
        for i, group in enumerate(by_token):
            got = group.swaps(send)
            if i + 1 < len(by_token):
                keep, *send = add_up(keep, got, by_token[i + 1].size, F32, "recon")
            else:
                keep, *send = split_columns(keep, got, by_feature, found[0][2:])
        got = by_feature.swaps(send)
        found += [norms(w, u, keep) for w, u in zip(held[1:], used[1:])]
        coefs, norm_rows, penalties = [list(x) for x in zip(*found)]
        rows = keep.shape[0]
        keep = with_penalty(keep, got[::-1], penalties)
        sums = deep.spread(keep)
        resid_t = turn(resid_all, keep)
        error_own = error_of(sums, resid_all, bias, by_feature, rows, [resid_t])

        others = by_feature.spread(error_own)[1:]
        first, height = gather(by_token, error_own), error_own.shape[0]
        back = first_back(first, height, held, by_feature)
        dec_grad, ready = first_outer(first, height, latents_t, coefs, held, by_feature, back)
        others = gather(by_token, stack(others, [ready])) if others else []
        dec_grad, enc_grad, bias_grad, column_sum, loss = gradients(
            first, others, height, resid_t, preact, latents_t, coefs, held, norm_rows, dec_grad, back, by_feature
        )
        return (enc_grad, bias_grad.reshape(-1), dec_grad, column_sum, loss.reshape(()))

    return body


def solution(mesh):
    placed = (
        P("dp", "fsdp"),
        P("fsdp", None),
        P(("dp", "fsdp"), None),
        P(),
        P(None, ("dp", "fsdp")),
        P(("dp", "fsdp")),
        P(("dp", "fsdp"), None),
        P(),
    )
    return jax.shard_map(
        make_body(mesh),
        mesh=mesh,
        in_specs=placed,
        out_specs=(P(None, ("dp", "fsdp")), P(("dp", "fsdp")), P(("dp", "fsdp"), None), P(), P()),
        check_vma=False,
    )
```

```python
import functools
import itertools
import math

import jax
import jax.numpy as jnp
from jax import lax
from jax.experimental import pallas as pl
from jax.experimental.pallas import tpu as pltpu
from jax.sharding import PartitionSpec as P

SPARSITY = 0.25
SMOOTHING = 0.1
EPSILON = 1e-06
F32 = jnp.float32
BF16 = jnp.bfloat16
LANES = 128


class Split:
    def __init__(self, axis, inner, size):
        self.axis, self.inner, self.size = axis, inner, size

    def place(self):
        return (lax.axis_index(self.axis) // self.inner) % self.size


class Group:
    def __init__(self, mesh, *splits):
        self.lengths = {axis: mesh.shape[axis] for axis in ("dp", "fsdp")}
        self.splits = splits
        self.size = math.prod(s.size for s in splits)
        self.keys = list(itertools.product(*(range(s.size) for s in splits)))

    def swap(self, x, key):
        pairs = []
        for d in range(self.lengths["dp"]):
            for f in range(self.lengths["fsdp"]):
                to = {"dp": d, "fsdp": f}
                for split, k in zip(self.splits, key):
                    a = (to[split.axis] // split.inner) % split.size
                    to[split.axis] += ((a ^ k) - a) * split.inner
                width = self.lengths["fsdp"]
                pairs.append((d * width + f, to["dp"] * width + to["fsdp"]))
        return lax.ppermute(x, ("dp", "fsdp"), pairs)

    def swaps(self, pieces):
        return [self.swap(p, key) for p, key in zip(pieces, self.keys[1:])]

    def spread(self, x):
        return [x] + [self.swap(x, key) for key in self.keys[1:]]


def block_of(total, most):
    return max(b for b in range(LANES, most + 1, LANES) if total % b == 0)


def resident(count):
    return [pl.BlockSpec(memory_space=pltpu.VMEM)] * count


def anywhere(count):
    return [pl.BlockSpec(memory_space=pl.ANY)] * count


def in_hbm(x):
    return pltpu.with_memory_space_constraint(x, pltpu.HBM)


def in_vmem(x):
    return pltpu.with_memory_space_constraint(x, pltpu.VMEM)


def params(megabytes):
    return pltpu.CompilerParams(vmem_limit_bytes=megabytes * 1024 * 1024)


def cost(flops, count):
    return pl.CostEstimate(flops=flops, bytes_accessed=count, transcendentals=0)


def struct(shape, kind):
    return jax.ShapeDtypeStruct(shape, kind)


def small(kernel, outs, *args, name):
    count = sum(x.size * x.dtype.itemsize for x in args) + sum(o.size * o.dtype.itemsize for o in outs)
    return pl.pallas_call(
        kernel,
        in_specs=resident(len(args)),
        out_specs=resident(len(outs)),
        out_shape=list(outs),
        compiler_params=params(6),
        cost_estimate=cost(count, count),
        name=name,
    )(*args)


def project(heads, weight, resid, gain, bias, deep, side):
    tokens = heads.shape[0]
    features = weight.shape[1]
    rows = tokens // side.size
    own = rows // deep.size
    quarter = features // deep.size
    wide = block_of(features, 1152)
    steps = features // wide

    def kernel(*refs):
        sources, outs = refs[:5], refs[5 : 8 + side.size]
        heads, weight, resid, gain, bias, sems = refs[8 + side.size :]
        packed, gain_row, bias_row, keep, *send = outs
        smalls = [
            pltpu.make_async_copy(source, here, sems.at[i])
            for i, (source, here) in enumerate([(sources[0], heads), *zip(sources[2:], (resid, gain, bias))])
        ]
        blocks = []
        for i in range(steps):
            at = pl.ds(i * wide, wide)
            blocks.append(pltpu.make_async_copy(sources[1].at[:, at], weight.at[:, at], sems.at[4 + i]))
        for copy in smalls[:1] + blocks + smalls[1:]:
            copy.start()

        to = lax.broadcasted_iota(jnp.int32, (tokens, tokens), 0)
        source = lax.broadcasted_iota(jnp.int32, (tokens, tokens), 1)
        across = lax.shift_right_logical(to, rows.bit_length() - 1) ^ side.place()
        down = (lax.shift_right_logical(to, own.bit_length() - 1) & (deep.size - 1)) ^ deep.place()
        wanted = (down * side.size + across) * own + (to & (own - 1))
        pick = jnp.where(source == wanted, 1.0, 0.0).astype(BF16)
        smalls[0].wait()
        turned = jnp.dot(pick, heads[...], preferred_element_type=F32).astype(BF16)
        for i, block in enumerate(blocks):
            block.wait()
            at = slice(i * wide, (i + 1) * wide)
            part = jnp.dot(turned, weight[:, at], preferred_element_type=F32)
            keep[:, at] = part[:rows]
            for k in range(1, side.size):
                send[k - 1][:, at] = part[k * rows : (k + 1) * rows].astype(BF16)
        for copy in smalls[1:]:
            copy.wait()
        values = resid[...].astype(F32)
        pieces = [values[:, q * quarter : (q + 1) * quarter] for q in range(deep.size)]
        packed[...] = jnp.concatenate(pieces, axis=0).astype(BF16)
        gain_row[...] = gain[...].reshape(1, features)
        bias_row[...] = bias[...].reshape(1, features)

    args = (heads, weight, resid, gain, bias)
    return pl.pallas_call(
        kernel,
        in_specs=anywhere(5),
        out_specs=resident(3 + side.size),
        out_shape=[struct((rows, quarter), BF16), struct((1, features), F32), struct((1, features), F32)]
        + [struct((rows, features), F32)]
        + [struct((rows, features), BF16)] * (side.size - 1),
        scratch_shapes=[pltpu.VMEM(x.shape, x.dtype) for x in args] + [pltpu.SemaphoreType.DMA((4 + steps,))],
        compiler_params=params(12),
        cost_estimate=cost(2 * tokens * weight.size, 2 * weight.size),
        name="project",
    )(*[in_hbm(x) for x in args])


def add_up(keep, got, parts, kind, name, beside=None, after=()):
    rows, columns = keep.shape
    part = rows // parts
    extra = [] if beside is None else [beside]
    width = columns + sum(b.shape[1] for b in extra)

    def kernel(*refs):
        ins, outs = refs[: 1 + len(got)], refs[-parts:]
        for p in range(parts):
            at = slice(p * part, (p + 1) * part)
            total = ins[0][at, :]
            for g in ins[1:]:
                total = total + g[at, :].astype(F32)
            outs[p][:, :columns] = total.astype(outs[p].dtype)
        if extra:
            outs[0][:, columns:] = refs[1 + len(got)][...]

    outs = [struct((part, width), kind)] + [struct((part, columns), BF16)] * (parts - 1)
    return small(kernel, outs, keep, *got, *extra, *after, name=name)


def group_sum(parts, own):
    size = len(parts)
    terms = []
    for k, part in enumerate(parts):
        pieces = [part[(j ^ k) * own : ((j ^ k) + 1) * own, :] for j in range(size)]
        terms.append(jnp.concatenate(pieces, axis=0) if size > 1 else part)
    while len(terms) > 1:
        half = len(terms) // 2
        terms = [terms[i] + terms[i + half] for i in range(half)]
    return terms[0]


def residual(parts, gain, after):
    rows = parts[0].shape[0]
    features = gain.shape[1]
    count = len(parts)
    own, quarter = rows // count, features // count
    parts, places = in_turn(parts)

    def kernel(*refs):
        sums, gain, out = [refs[i] for i in places], refs[count], refs[-1]
        projected = group_sum([p[:, :features].astype(F32) for p in sums], own)
        scale = lax.rsqrt(jnp.mean(projected * projected, axis=-1, keepdims=True) + EPSILON)
        packed = [p[:, features:].astype(F32) for p in sums]
        for q in range(count):
            at = slice(q * quarter, (q + 1) * quarter)
            before = jnp.concatenate([p[q * own : (q + 1) * own, :] for p in packed], axis=0)
            out[:, at] = (before + projected[:, at] * scale * gain[:, at]).astype(BF16)

    return small(kernel, [struct((rows, features), BF16)], *parts, gain, *after, name="residual")[0]


def chunk_at(group, key, width):
    place = 0
    for split, k in zip(group.splits, key):
        place = place * split.size + (split.place() ^ k)
    return pl.multiple_of(place * width, LANES)


def split_columns(keep, got, group, after):
    rows, columns = keep.shape
    width = columns // group.size

    def kernel(*refs):
        ins, outs = refs[: 1 + len(got)], refs[-group.size :]
        for key, out in zip(group.keys, outs):
            at = pl.ds(chunk_at(group, key, width), width)
            total = ins[0][:, at]
            for g in ins[1:]:
                total = total + g[:, at].astype(F32)
            out[...] = total.astype(out.dtype)

    outs = [struct((rows, width), F32)] + [struct((rows, width), BF16)] * (group.size - 1)
    return small(kernel, outs, keep, *got, *after, name="recon")


def fewest(rows):
    return 8 if rows % 8 == 0 else rows


def lay(out, x):
    rows, width = x.shape
    height = out.shape[0]
    for i in range(rows // height):
        out[:, i * width : (i + 1) * width] = x[i * height : (i + 1) * height, :]


def unlaid(x, rows, width):
    height = x.shape[0]
    return jnp.concatenate([x[:, i * width : (i + 1) * width] for i in range(rows // height)], axis=0)


def put_number(out, at, value):
    high = value.astype(BF16)
    low = (value - high.astype(F32)).astype(BF16)
    half = LANES // 2
    out[:, at : at + half] = jnp.broadcast_to(high, (out.shape[0], half))
    out[:, at + half : at + LANES] = jnp.broadcast_to(low, (out.shape[0], half))


def get_number(x, at):
    half = LANES // 2
    return x[:1, at : at + 1].astype(F32) + x[:1, at + half : at + half + 1].astype(F32)


def with_penalty(keep, got, penalties):
    rows, width = keep.shape

    def kernel(*refs):
        ins, numbers, out = refs[: 1 + len(got)], refs[1 + len(got) : -1], refs[-1]
        total = ins[0][...]
        for g in ins[1:]:
            total = total + g[...].astype(F32)
        lay(out, total.astype(BF16))
        penalty = numbers[0][:1, :1]
        for n in numbers[1:]:
            penalty = penalty + n[:1, :1]
        put_number(out, length, penalty)

    height = fewest(rows)
    length = rows // height * width
    return small(kernel, [struct((height, length + LANES), BF16)], keep, *got, *penalties, name="recon")[0]


def tree(terms):
    terms = list(terms)
    while len(terms) > 1:
        half = len(terms) // 2
        terms = [terms[i] + terms[i + half] for i in range(half)]
    return terms[0]


def in_turn(parts):
    order = [0, 1, 3, 2] if len(parts) == 4 else list(range(len(parts)))
    return [parts[i] for i in order], [order.index(i) for i in range(len(parts))]


def error_of(parts, resid, bias, group, rows, after):
    parts, places = in_turn(parts)
    height, length = parts[0].shape
    length -= LANES
    width = resid.shape[1] // group.size

    def kernel(*refs):
        sums, resid, bias, out = refs[: len(parts)], refs[len(parts)], refs[len(parts) + 1], refs[-1]
        at = pl.ds(chunk_at(group, group.keys[0], width), width)
        sums = [sums[i] for i in places]
        total = unlaid(tree([p[:, :length].astype(F32) for p in sums]), rows, width)
        lay(out, (total + bias[:, at] - resid[:rows, at].astype(F32)).astype(BF16))
        put_number(out, length, tree([get_number(p, length) for p in sums]))

    return small(kernel, [struct((height, length + LANES), BF16)], *parts, resid, bias, *after, name="error")[0]


def stack(pieces, after=()):
    rows, columns = sum(p.shape[0] for p in pieces), pieces[0].shape[1]

    def kernel(*refs):
        row = 0
        for ref in refs[: len(pieces)]:
            refs[-1][row : row + ref.shape[0], :] = ref[...]
            row += ref.shape[0]

    return small(kernel, [struct((rows, columns), pieces[0].dtype)], *pieces, *after, name="stack")[0]


def gather(stages, *pieces):
    pieces = list(pieces)
    for group in reversed(stages):
        if len(pieces) > 4:
            pieces = [stack(pieces)]
        pieces = pieces + [group.swap(p, key) for key in group.keys[1:] for p in pieces]
    return pieces


def copy_rows(source, first, here, sems, start, step=384):
    rows = here.shape[0]
    step = max(b for b in range(16, step + 1, 16) if rows % b == 0)
    return [
        pltpu.make_async_copy(source.at[pl.ds(first + r, step)], here.at[pl.ds(r, step)], sems.at[start + r // step])
        for r in range(0, rows, step)
    ]


MOST_COPIES = 32


def in_order(copies, act):
    def body(_, carry):
        for copy in copies:
            copy.start() if act == "start" else copy.wait()
        return carry

    lax.fori_loop(0, jnp.minimum(lax.axis_index("fsdp") + 1, 1), body, 0)


def load(items, after, name):
    def kernel(*refs):
        sources, results, sems = refs[: len(items)], refs[len(items) + 1 : -1], refs[-1]
        copies = []
        for source, here, (_, first, _) in zip(sources, results, items):
            copies += copy_rows(source, first, here, sems, len(copies))
        for copy in copies:
            copy.start()
        results[-1][...] = jnp.zeros_like(results[-1])
        for copy in copies:
            copy.wait()

    return pl.pallas_call(
        kernel,
        in_specs=anywhere(len(items)) + resident(1),
        out_specs=resident(len(items) + 1),
        out_shape=[pltpu.VMEM((rows, source.shape[1]), source.dtype) for source, _, rows in items]
        + [struct((8, LANES), F32)],
        scratch_shapes=[pltpu.SemaphoreType.DMA((MOST_COPIES,))],
        compiler_params=params(4),
        cost_estimate=cost(0, sum(2 * rows * source.shape[1] for source, _, rows in items)),
        name=name,
    )(*[in_hbm(item[0]) for item in items], after)


def norms(weights, usages, after):
    rows, features = weights.shape
    step = math.gcd(rows, 256)

    def kernel(weight, usage, after, coef, norm_row, penalty):
        total = jnp.zeros((1, 1), F32)
        for r in range(0, rows, step):
            at = slice(r, r + step)
            squares = jnp.zeros((step, LANES), F32)
            for c in range(0, features, LANES):
                w = weight[at, c : c + LANES].astype(F32)
                squares = squares + w * w
            norm = jnp.sqrt(jnp.sum(squares, axis=1, keepdims=True) + EPSILON)
            used = usage[at, :]
            coef[at, :] = SPARSITY * (used / norm)
            norm_row[:, at] = jnp.broadcast_to(norm, (step, LANES)).T[:1, :]
            total = total + jnp.sum(used * norm, axis=0, keepdims=True)
        penalty[...] = jnp.broadcast_to(total, penalty.shape)

    return pl.pallas_call(
        kernel,
        in_specs=resident(3),
        out_specs=resident(3),
        out_shape=[struct((rows, 1), F32), struct((1, rows), F32), struct((8, LANES), F32)],
        compiler_params=params(6),
        cost_estimate=cost(0, 6 * rows * features),
        name="norms",
    )(in_vmem(weights), usages, after)


def encode(parts, held, bias, dec_weight, first, cut, mask_of):
    starts = range(first, dec_weight.shape[0], cut)
    tokens = sum(p.shape[0] for p in parts)
    features = parts[0].shape[1]
    latents = held[0].shape[1]
    wide = block_of(latents, 256)

    def kernel(*refs):
        parts_in, weights = refs[: len(parts)], refs[len(parts) : len(parts) + len(held)]
        bias, source, preact, resid, *here, stacked, sems = refs[len(parts) + len(held) :]
        copies = []
        for start, piece in zip(starts, here):
            copies += copy_rows(source, start, piece, sems, len(copies))
        in_order(copies, "start")
        row = 0
        for part in parts_in:
            stacked[row : row + part.shape[0], :] = part[...]
            row += part.shape[0]
        to = lax.broadcasted_iota(jnp.int32, (tokens, tokens), 0)
        source_row = lax.broadcasted_iota(jnp.int32, (tokens, tokens), 1)
        pick = jnp.where(source_row == (to ^ mask_of()), 1.0, 0.0).astype(BF16)
        block = block_of(features, 512)
        for c in range(0, features, block):
            at = slice(c, c + block)
            resid[:, at] = jnp.dot(pick, stacked[:, at], preferred_element_type=F32).astype(BF16)
        row = bias[...].reshape(1, latents)
        for c in range(0, latents, wide):
            at = slice(c, c + wide)
            total, start = row[:, at], 0
            for w in weights:
                span = w.shape[0]
                total = total + jnp.dot(resid[:, start : start + span], w[:, at], preferred_element_type=F32)
                start += span
            preact[:, at] = total
        in_order(copies, "wait")

    return pl.pallas_call(
        kernel,
        in_specs=resident(len(parts) + len(held) + 1) + anywhere(1),
        out_specs=resident(2 + len(starts)),
        out_shape=[struct((tokens, latents), F32), struct((tokens, features), BF16)]
        + [pltpu.VMEM((cut, features), BF16)] * len(starts),
        scratch_shapes=[pltpu.VMEM((tokens, features), BF16), pltpu.SemaphoreType.DMA((MOST_COPIES,))],
        compiler_params=params(6),
        cost_estimate=cost(2 * tokens * features * latents, 2 * tokens * features),
        name="encode",
    )(*parts, *[in_vmem(w) for w in held], bias, in_hbm(dec_weight))


def decode(preact, held, parts):
    tokens, latents = preact.shape
    features = held[0].shape[1]
    kept = tokens // parts
    sent = max(tokens - kept, 8)
    count = len(held)
    wide = block_of(features, 512)
    sizes = [w.shape[0] for w in held]
    step = math.gcd(*sizes, 256)

    def kernel(preact, *refs):
        weights, keep, send, latents_t = refs[:count], *refs[count : count + 3]
        usages, latents_b = refs[count + 3 : -1], refs[-1]
        for i, (p, r) in enumerate(row_blocks(weights, step)):
            at = slice(i * step, (i + 1) * step)
            value = jnp.maximum(preact[:, at], 0.0)
            latents_b[:, at] = value.astype(BF16)
            turned = value.T
            latents_t[at, :] = turned.astype(BF16)
            usages[p][r : r + step, :] = jnp.sum(turned, axis=1, keepdims=True)
        for c in range(0, features, wide):
            at = slice(c, c + wide)
            part, start = None, 0
            for w, span in zip(weights, sizes):
                term = jnp.dot(latents_b[:, start : start + span], w[:, at], preferred_element_type=F32)
                part = term if part is None else part + term
                start += span
            keep[:, at] = part[:kept]
            if kept < tokens:
                send[:, at] = part[kept:].astype(BF16)

    return pl.pallas_call(
        kernel,
        in_specs=resident(1 + count),
        out_specs=resident(3 + count),
        out_shape=[
            struct((kept, features), F32),
            struct((sent, features), BF16),
            struct((latents, tokens), BF16),
        ]
        + [struct((size, 1), F32) for size in sizes],
        scratch_shapes=[pltpu.VMEM((tokens, latents), BF16)],
        compiler_params=params(6),
        cost_estimate=cost(2 * tokens * features * latents, 6 * tokens * features),
        name="decode",
    )(preact, *[in_vmem(w) for w in held])


def turn(x, after):
    def kernel(x, after, out):
        out[...] = x[...].astype(F32).T.astype(BF16)

    return small(kernel, [struct(x.shape[::-1], BF16)], x, after, name="turn")[0]


def row_blocks(weights, rows):
    return [(p, r) for p, w in enumerate(weights) for r in range(0, w.shape[0], rows)]


def fold(x):
    n = x.shape[0]
    while n > 1 and n % 2 == 0:
        n //= 2
        x = x[:n] + x[n:]
    return x if n == 1 else jnp.sum(x, axis=0, keepdims=True)


def row_blocks(weights, rows):
    return [(p, r) for p, w in enumerate(weights) for r in range(0, w.shape[0], rows)]


def units(refs, height):
    return [ref.at[pl.ds(r, height)] for ref in refs for r in range(0, ref.shape[0], height)]


def assemble(messages, error, width):
    height = messages[0].shape[0]
    groups = error.shape[0] // len(messages) // height
    for i, message in enumerate(messages):
        for g in range(groups):
            at = (i * groups + g) * height
            error[at : at + height, :] = message[:, g * width : (g + 1) * width]


def spans(width):
    wide = min(width, 512)
    return [(c, min(wide, width - c)) for c in range(0, width, wide)]


def whole_tiles(width):
    return width // 256 * 256


def outer(latents_t, error, coef, weight):
    return (jnp.dot(latents_t, error, preferred_element_type=F32) + coef * weight.astype(F32)).astype(BF16)


def back_product(error, weight):
    return lax.dot_general(error, weight, (((1,), (1,)), ((), ())), preferred_element_type=F32)


def first_gradients(parts, height, latents_t, coefs, weights, group):
    latents, tokens = latents_t.shape
    features = weights[0].shape[1]
    width = features // group.size
    count = len(weights)
    rows = math.gcd(*[w.shape[0] for w in weights], 256)

    def kernel(*refs):
        pieces, refs = refs[: len(parts)], refs[len(parts) :]
        coef, held = refs[:count], refs[count : 2 * count]
        latents_t, dec_grad, back, error, stage, sems = refs[2 * count :]
        columns = chunk_at(group, group.keys[0], width)
        assemble(units(pieces, height), error, width)
        copies = []
        for i, (p, r) in enumerate(row_blocks(held, rows)):
            at, inside = slice(i * rows, (i + 1) * rows), slice(r, r + rows)
            for c, wide in spans(width):
                over = pl.ds(pl.multiple_of(columns + c, LANES), wide)
                stage[at, c : c + wide] = outer(
                    latents_t[at, :], error[:, c : c + wide], coef[p][inside, :], held[p][inside, over]
                )
            at = pl.ds(i * rows, rows)
            copies.append(
                pltpu.make_async_copy(stage.at[at], dec_grad.at[at, pl.ds(columns, width)], sems.at[i])
            )
        in_order(copies, "start")
        for i, (p, r) in enumerate(row_blocks(held, rows)):
            weight = held[p][r : r + rows, pl.ds(columns, width)]
            back[:, i * rows : (i + 1) * rows] = back_product(error[...], weight)
        in_order(copies, "wait")

    return pl.pallas_call(
        kernel,
        in_specs=resident(len(parts) + 2 * count + 1),
        out_specs=anywhere(1) + resident(1),
        out_shape=[struct((latents, features), BF16), struct((tokens, latents), F32)],
        scratch_shapes=[
            pltpu.VMEM((tokens, width), BF16),
            pltpu.VMEM((latents, width), BF16),
            pltpu.SemaphoreType.DMA((latents // rows,)),
        ],
        compiler_params=params(10),
        cost_estimate=cost(4 * tokens * width * latents, 4 * width * latents),
        name="first_gradients",
    )(*parts, *coefs, *[in_vmem(w) for w in weights], latents_t)


def gradients(first, others, height, resid_t, preact, latents_t, coefs, weights, norm_rows, dec_grad, back, group):
    tokens, latents = preact.shape
    features = weights[0].shape[1]
    width = features // group.size
    count, size = len(weights), group.size
    pieces = len(first)
    rows = math.gcd(*[w.shape[0] for w in weights], 256)
    span = math.gcd(latents, 512)
    deep = block_of(features, 1152)
    dec_slots, enc_slots = 3, 6
    main = whole_tiles(width)
    half = math.gcd(span, 256)
    flat = first + others

    def kernel(*refs):
        chunks = [units(refs[:pieces], height)]
        chunks += [units(refs[pieces : len(flat)], height)[k :: size - 1] for k in range(size - 1)]
        refs = refs[len(flat) :]
        coef, held, norm_row, refs = refs[:count], refs[count : 2 * count], refs[2 * count : 3 * count], refs[3 * count :]
        (resid_t, preact, latents_t, back, _, dec_grad, enc_grad, bias_grad, column_sum, loss,
         error, ends, pulled, sums, dec_stage, enc_stage, dec_sem, enc_sem) = refs
        columns = [chunk_at(group, key, width) for key in group.keys]
        for k in range(size):
            assemble(chunks[k], error.at[k], width)
        for k in range(1, size):
            if main < width:
                ends[:, (k - 1) * (width - main) : k * (width - main)] = error[k, :, main:]
        where = row_blocks(held, rows)
        dec_copies, enc_copies = [], []

        def products(i):
            p, r = where[i]
            at, inside = slice(i * rows, (i + 1) * rows), slice(r, r + rows)
            total = back[:, at]
            for k in range(1, size):
                for c, wide in spans(main):
                    part = error[k, :, c : c + wide]
                    weight = held[p][inside, pl.ds(pl.multiple_of(columns[k] + c, LANES), wide)]
                    dec_stage[i % dec_slots, k - 1, :, c : c + wide] = outer(
                        latents_t[at, :], part, coef[p][inside, :], weight
                    )
                    total = total + back_product(part, weight)
            if main < width and size > 1:
                weight = jnp.concatenate(
                    [
                        held[p][inside, pl.ds(pl.multiple_of(columns[k] + main, LANES), width - main)]
                        for k in range(1, size)
                    ],
                    axis=1,
                )
                product = outer(latents_t[at, :], ends[...], coef[p][inside, :], weight)
                for k in range(1, size):
                    over = slice((k - 1) * (width - main), k * (width - main))
                    dec_stage[i % dec_slots, k - 1, :, main:] = product[:, over]
                total = total + back_product(ends[...], weight)
            total = (total + SPARSITY * norm_row[p][:, inside]) * jax.nn.sigmoid(preact[:, at] / SMOOTHING)
            bias_grad[:, at] = jnp.sum(total, axis=0, keepdims=True)
            pulled[:, at] = total.astype(BF16)

        def send_rows(i):
            slot = i % dec_slots
            for k in range(1, size):
                copy = pltpu.make_async_copy(
                    dec_stage.at[slot, k - 1],
                    dec_grad.at[pl.ds(i * rows, rows), pl.ds(columns[k], width)],
                    dec_sem.at[slot, k - 1],
                )
                copy.start()
                dec_copies.append(copy)

        blocks = [(first, j) for first in range(0, latents, span) for j in range(0, features, deep)]

        def block(n):
            first, j = blocks[n]
            part = block_of(deep, 384)
            for r in range(0, deep, part):
                for c in range(0, span, half):
                    enc_stage[n % enc_slots, r : r + part, c : c + half] = jnp.dot(
                        resid_t[j + r : j + r + part, :],
                        pulled[:, first + c : first + c + half],
                        preferred_element_type=F32,
                    ).astype(BF16)

        def send_block(n):
            (first, j), slot = blocks[n], n % enc_slots
            copy = pltpu.make_async_copy(
                enc_stage.at[slot], enc_grad.at[pl.ds(j, deep), pl.ds(first, span)], enc_sem.at[slot]
            )
            copy.start()
            enc_copies.append(copy)

        def free_block(n):
            if n >= enc_slots:
                enc_copies[n - enc_slots].wait()

        each, per = span // rows, features // deep
        done = 0
        for i in range(latents // rows):
            if i >= dec_slots:
                for k in range(1, size):
                    dec_copies[(i - dec_slots) * (size - 1) + k - 1].wait()
            upto = min(done + -(-per // each), i // each * per)
            for n in range(done, upto):
                free_block(n)
            products(i)
            for n in range(done, upto):
                block(n)
            send_rows(i)
            for n in range(done, upto):
                send_block(n)
            done = upto
        for n in range(done, len(blocks)):
            free_block(n)
            block(n)
            send_block(n)

        squares, penalties = [], []
        for k in range(size):
            total = jnp.zeros((1, 1), F32)
            for c, wide in spans(width):
                e = error[k, :, c : c + wide].astype(F32)
                sums[:, pl.ds(pl.multiple_of(columns[k] + c, LANES), wide)] = fold(e)
                total = total + jnp.sum(fold(e * e), axis=1, keepdims=True)
            squares.append(total)
            penalties += [get_number(piece[...], piece.shape[1] - LANES) for piece in chunks[k]]
        column_sum[...] = sums[...].reshape(features)
        value = (0.5 * tree(squares) + SPARSITY * tree(penalties)) / (tokens * features)
        loss[0, 0] = jnp.sum(value)
        for copy in dec_copies[-dec_slots * (size - 1) :] + enc_copies[-enc_slots:]:
            copy.wait()

    return pl.pallas_call(
        kernel,
        in_specs=resident(len(flat) + 3 * count + 4) + anywhere(1),
        out_specs=anywhere(2) + resident(2) + [pl.BlockSpec(memory_space=pltpu.SMEM)],
        out_shape=[
            struct((latents, features), BF16),
            struct((features, latents), BF16),
            struct((1, latents), F32),
            struct((features,), F32),
            struct((1, 1), F32),
        ],
        scratch_shapes=[
            pltpu.VMEM((size, tokens, width), BF16),
            pltpu.VMEM((tokens, max(size - 1, 1) * max(width - main, LANES)), BF16),
            pltpu.VMEM((tokens, latents), BF16),
            pltpu.VMEM((1, features), F32),
            pltpu.VMEM((dec_slots, max(size - 1, 1), rows, width), BF16),
            pltpu.VMEM((enc_slots, deep, span), BF16),
            pltpu.SemaphoreType.DMA((dec_slots, max(size - 1, 1))),
            pltpu.SemaphoreType.DMA((enc_slots,)),
        ],
        input_output_aliases={len(flat) + 3 * count + 4: 0},
        compiler_params=params(18),
        cost_estimate=cost(6 * tokens * features * latents, 4 * features * latents),
        name="gradients",
    )(*flat, *coefs, *[in_vmem(w) for w in weights], *norm_rows, resid_t, preact, latents_t, back, dec_grad)


def make_body(mesh):
    dp, fsdp = mesh.shape["dp"], mesh.shape["fsdp"]
    cores = 2 if dp % 2 == 0 else 1
    depth = 4 if fsdp % 4 == 0 else 1
    core_split, across_split = Split("dp", 1, cores), Split("dp", cores, dp // cores)
    deep_split, side_split = Split("fsdp", fsdp // depth, depth), Split("fsdp", 1, fsdp // depth)
    core, deep, side = Group(mesh, core_split), Group(mesh, deep_split), Group(mesh, side_split)
    if across_split.size * side_split.size <= 4:
        by_token, by_feature = [core], Group(mesh, across_split, side_split)
    else:
        by_token, by_feature = [core, Group(mesh, across_split)], side
    stages = by_token + [by_feature]

    def body(attn_heads, out_proj, resid_pre, post_gain, enc_weight, enc_bias, dec_weight, dec_bias):
        own = resid_pre.shape[0]
        latents, features = dec_weight.shape
        cut = max(latents // 4, LANES)
        depth = features // 3

        def mask():
            place = 0
            for split in (across_split, side_split):
                shared = any(split is s for s in by_feature.splits)
                place = place * split.size + (split.place() if shared else 0)
            return (place * deep_split.size + deep_split.place()) * own

        packed, gain, bias, keep, *send = project(
            attn_heads, out_proj, resid_pre, post_gain, dec_bias, deep_split, side_split
        )
        got = side.swaps(send)
        enc_first, ready = load([(enc_weight, 0, depth)], send[0] if send else keep, "load_first")
        summed = add_up(keep, got, 1, BF16, "heads_y", packed, [ready])[0]
        sums = deep.spread(summed)
        enc_second, enc_third, dec_first, ready = load(
            [(enc_weight, depth, depth), (enc_weight, 2 * depth, depth), (dec_weight, 0, cut)], summed, "load_second"
        )
        resid_own = residual(sums, gain, [ready])
        near = by_feature.spread(resid_own)
        held, ready = [dec_first], []
        if latents == 4 * cut:
            dec_next, *ready = load([(dec_weight, cut, cut)], resid_own, "load_third")
            held.append(dec_next)
        near = near[:1] + [stack(near[1:], ready)] * (len(near) > 1)
        resid_parts = gather(by_token, *near)

        preact, resid_all, *dec_last = encode(
            resid_parts, [enc_first, enc_second, enc_third], enc_bias, dec_weight, cut * len(held), cut, mask
        )
        held += dec_last
        keep, send, latents_t, *used = decode(preact, held, core.size)
        send = [send]
        found = [norms(held[0], used[0], send[0])]
        for i, group in enumerate(by_token):
            got = group.swaps(send)
            if i + 1 < len(by_token):
                keep, *send = add_up(keep, got, by_token[i + 1].size, F32, "recon")
            else:
                keep, *send = split_columns(keep, got, by_feature, found[0][2:])
        got = by_feature.swaps(send)
        found += [norms(w, u, keep) for w, u in zip(held[1:], used[1:])]
        coefs, norm_rows, penalties = [list(x) for x in zip(*found)]
        rows = keep.shape[0]
        keep = with_penalty(keep, got[::-1], penalties)
        sums = deep.spread(keep)
        resid_t = turn(resid_all, keep)
        error_own = error_of(sums, resid_all, bias, by_feature, rows, [resid_t])

        others = by_feature.spread(error_own)[1:]
        first, height = gather(by_token, error_own), error_own.shape[0]
        dec_grad, back = first_gradients(first, height, latents_t, coefs, held, by_feature)
        others = gather(by_token, stack(others, [back])) if others else []
        dec_grad, enc_grad, bias_grad, column_sum, loss = gradients(
            first, others, height, resid_t, preact, latents_t, coefs, held, norm_rows, dec_grad, back, by_feature
        )
        return (enc_grad, bias_grad.reshape(-1), dec_grad, column_sum, loss.reshape(()))

    return body


def solution(mesh):
    placed = (
        P("dp", "fsdp"),
        P("fsdp", None),
        P(("dp", "fsdp"), None),
        P(),
        P(None, ("dp", "fsdp")),
        P(("dp", "fsdp")),
        P(("dp", "fsdp"), None),
        P(),
    )
    return jax.shard_map(
        make_body(mesh),
        mesh=mesh,
        in_specs=placed,
        out_specs=(P(None, ("dp", "fsdp")), P(("dp", "fsdp")), P(("dp", "fsdp"), None), P(), P()),
        check_vma=False,
    )
```
